32 devices in a mesh: dp: 2 (over core), row: 4 (over y, x), col: 4 (over z).
Axes of the slice: x: 2, y: 2, z: 4, core: 2. Of those that a mesh axis runs over, the one named last changes fastest.
Arguments:
- block_input: bfloat16 [20480, 2048], P(('dp', 'col'), 'row'), may hold values from -45 to 45
- cotangent: bfloat16 [20480, 2048], P(('dp', 'col'), 'row'), may hold values from -6 to 6
- attn_gain: bfloat16 [2048], P('row'), may hold values from 0.25 to 1.75
- attn_shift: bfloat16 [2048], P('row'), may hold values from -0.14941406 to 0.14941406
- query_weight: bfloat16 [2048, 2048], P('row', 'col'), may hold values from -0.125 to 0.125
- query_bias: bfloat16 [2048], P('col'), may hold values from -2.5 to 2.5
- keyval_weight: bfloat16 [2048, 256], P('row'), may hold values from -0.125 to 0.125
- value_bias: bfloat16 [128], replicated, may hold values from -0.14941406 to 0.14941406
- output_weight: bfloat16 [2048, 2048], P('col', 'row'), may hold values from -6 to 6
- output_bias: bfloat16 [2048], P('row'), may hold values from -4 to 4
- mlp_gain: bfloat16 [2048], P('row'), may hold values from 0.25 to 1.75
- mlp_shift: bfloat16 [2048], P('row'), may hold values from -1.5 to 1.5
- expand_weight: bfloat16 [2048, 8192], P('row', 'col'), may hold values from -0.125 to 0.125
- expand_bias: bfloat16 [8192], P('col'), may hold values from -2.5 to 2.5
- shrink_weight: bfloat16 [8192, 2048], P('col', 'row'), may hold values from -0.0625 to 0.0625
- shrink_bias: bfloat16 [2048], P('row'), may hold values from -4 to 4
- seg_parent: int32 [4, 13], P('dp'), may hold values from -1 to 12, as said below
- seg_start: int32 [4, 13], P('dp'), may hold values from 0 to 4864, as said below
- seg_length: int32 [4, 13], P('dp'), may hold values from 256 to 2048, as said below
Outputs:
- block_output: bfloat16 [20480, 2048], P(('dp', 'col'), 'row')
- input_grad: float32 [20480, 2048], P(('dp', 'col'), 'row')
- attn_gain_grad: float32 [2048], P('row')
- attn_shift_grad: float32 [2048], P('row')
- query_weight_grad: float32 [2048, 2048], P('row', 'col')
- query_bias_grad: float32 [2048], P('col')
- keyval_weight_grad: float32 [2048, 256], P('row')
- value_bias_grad: float32 [128], replicated
- output_weight_grad: float32 [2048, 2048], P('col', 'row')
- output_bias_grad: float32 [2048], P('row')
- mlp_gain_grad: float32 [2048], P('row')
- mlp_shift_grad: float32 [2048], P('row')
- expand_weight_grad: float32 [2048, 8192], P('row', 'col')
- expand_bias_grad: float32 [8192], P('col')
- shrink_weight_grad: float32 [8192, 2048], P('col', 'row')
- shrink_bias_grad: float32 [2048], P('row')
The draws below stay inside these ranges and needn't reach their ends.
Inputs may be any that keep to these rules, and one draw needn't show every extreme that they name: `seg_parent`: each tree has 13 segments in slots listed in memory order: one trunk (parent -1), 4 branches whose parent is the trunk and 2 leaves under each branch; the order of the slots is drawn, except that the last slot of every tree holds a branch. `seg_start`: segments are contiguous and tile the tree's 5120 tokens in slot order. `seg_length`: the trunk has 2048 tokens, every branch and leaf 256.
All inputs are finite; a program needn't handle non-finite values.
Results may differ from the reference program's by a relative error of at most 0.02.
Values may be sent and summed in bfloat16 or wider, within the bound.
No kernel may reach another device: no remote copies, remote signals or barrier semaphores. Data moves between devices by JAX's collectives and lax.ppermute only.
A program may use at most 448 MiB of HBM per device.

```python
import math
import jax
import jax.numpy as jnp
from jax import lax

D = 2048
H = 16
HD = 128
FF = 8192
TRUNK = 2048
SEG_LEN = 256
NBR = 4
NLEAF = 2
SEGS = 13
TREE_TOK = 5120
TREES = 4
TOKENS = 20480


def draw_block_input(key, part):
    draw_keys = jax.random.split(jax.random.fold_in(key, 11), 4)
    row_scale = jnp.exp(jax.random.uniform(draw_keys[0], (TOKENS, 1), jnp.float32, math.log(0.3), math.log(3.0)))
    col_scale = jnp.exp(jax.random.uniform(draw_keys[1], (1, D), jnp.float32, math.log(0.4), math.log(2.5)))
    base_vals = jnp.clip(jax.random.normal(draw_keys[2], (TOKENS, D), jnp.float32), -5.0, 5.0)
    offsets = jnp.clip(0.3 * jax.random.normal(draw_keys[3], (TOKENS, 1), jnp.float32), -1.5, 1.5)
    return (row_scale * (base_vals * col_scale + offsets)).astype(jnp.bfloat16)


def tree_layout(key):
    tree_keys = jax.random.split(jax.random.fold_in(key, 5), TREES)

    def one_tree(tree_key):
        drawn = jax.random.permutation(tree_key, SEGS).astype(jnp.int32)
        branch_pos = jnp.argsort(drawn)[1].astype(jnp.int32)
        last_val = drawn[SEGS - 1]
        order = drawn.at[branch_pos].set(last_val).at[SEGS - 1].set(1)
        canon = jnp.arange(SEGS, dtype=jnp.int32)
        parent_canon = jnp.where(canon == 0, -1, jnp.where(canon <= NBR, 0, 1 + (canon - 1 - NBR) // NLEAF))
        length_canon = jnp.where(canon == 0, TRUNK, SEG_LEN).astype(jnp.int32)
        slot_of = jnp.argsort(order).astype(jnp.int32)
        parent_by_slot = parent_canon[order]
        parents = jnp.where(parent_by_slot < 0, -1, slot_of[jnp.maximum(parent_by_slot, 0)])
        lengths = length_canon[order]
        starts = jnp.cumsum(lengths) - lengths
        return (parents.astype(jnp.int32), starts.astype(jnp.int32), lengths.astype(jnp.int32))
    return jax.vmap(one_tree)(tree_keys)


def draw_seg_parent(key, part):
    return tree_layout(key)[0]


def draw_seg_start(key, part):
    return tree_layout(key)[1]


def draw_seg_length(key, part):
    return tree_layout(key)[2]


def level_of(stream_key, extent, cuts, low, high):
    def one(axis_at, blocks):
        draws = jax.random.uniform(jax.random.fold_in(jax.random.fold_in(stream_key, 6), axis_at), (blocks,), jnp.float32, low / len(cuts), high / len(cuts))
        return jnp.repeat(jnp.exp(draws), extent[axis_at] // blocks).reshape((-1,) + (1,) * (len(extent) - axis_at - 1))

    gain = one(*cuts[0])
    for cut in cuts[1:]:
        gain = gain * one(*cut)
    return gain


def normal_values(rng, extent, scale, most, cuts=(), kind=jnp.bfloat16):
    factor_of = level_of(rng, extent, cuts, -0.22, 0.18) if cuts else 1.0
    entries = jax.random.normal(rng, extent, jnp.float32) * scale * factor_of
    return jnp.minimum(jnp.maximum(entries, -most), most).astype(kind)


def setup_inputs(seed: int = 0) -> dict:
    seeds = jax.random.split(jax.random.key(seed), 20)
    return {
        "block_input": draw_block_input(jax.random.fold_in(seeds[19], 71), 0),
        "cotangent": normal_values(seeds[1], (TOKENS, D), 1.0, 6.0, ((0, 8), (1, 4))),
        "attn_gain": jnp.clip(1.0 + 0.15 * jax.random.normal(seeds[2], (D,), jnp.float32), 0.25, 1.75).astype(jnp.bfloat16),
        "attn_shift": normal_values(seeds[3], (D,), 0.03, 0.14941406, ((0, 4),)),
        "query_weight": normal_values(seeds[4], (D, D), D ** -0.5, 0.125, ((0, 4), (1, 4))),
        "query_bias": normal_values(seeds[5], (D,), 0.5, 2.5, ((0, 4),)),
        "keyval_weight": normal_values(seeds[6], (D, 2 * HD), D ** -0.5, 0.125, ((0, 4),)),
        "value_bias": normal_values(seeds[7], (HD,), 0.03, 0.14941406),
        "output_weight": normal_values(seeds[8], (D, D), (max(4 * D // TREE_TOK, 1)) ** -0.5, 6.0, ((0, 4), (1, 4))),
        "output_bias": normal_values(seeds[9], (D,), 1.0, 4.0, ((0, 4),)),
        "mlp_gain": jnp.clip(1.0 + 0.15 * jax.random.normal(seeds[10], (D,), jnp.float32), 0.25, 1.75).astype(jnp.bfloat16),
        "mlp_shift": normal_values(seeds[11], (D,), 0.3, 1.5, ((0, 4),)),
        "expand_weight": normal_values(seeds[12], (D, FF), D ** -0.5, 0.125, ((0, 4), (1, 4))),
        "expand_bias": normal_values(seeds[13], (FF,), 0.5, 2.5, ((0, 4),)),
        "shrink_weight": normal_values(seeds[14], (FF, D), FF ** -0.5, 0.0625, ((0, 4), (1, 4))),
        "shrink_bias": normal_values(seeds[15], (D,), 1.0, 4.0, ((0, 4),)),
        "seg_parent": draw_seg_parent(jax.random.fold_in(seeds[19], 71), 0),
        "seg_start": draw_seg_start(jax.random.fold_in(seeds[19], 71), 0),
        "seg_length": draw_seg_length(jax.random.fold_in(seeds[19], 71), 0),
    }


@jax.custom_vjp
def low(v):
    return lax.optimization_barrier(v.astype(jnp.bfloat16)).astype(jnp.float32)

@jax.custom_vjp
def low_back(v):
    return v

def low_keep(v):
    return (low(v), None)

def low_pass(kept, grad):
    return (grad,)

def back_keep(v):
    return (v, None)

def back_low(kept, grad):
    return (low(grad),)
low.defvjp(low_keep, low_pass)
low_back.defvjp(back_keep, back_low)
EPSILON = 1e-05

def matmul(first_arr, second_arr):
    return jnp.dot(first_arr, second_arr, precision=lax.Precision.HIGHEST)

def layer_norm(values_in, gain_vec, shift_vec):
    row_mean = lax.optimization_barrier(jnp.mean(values_in, axis=-1, keepdims=True))
    centred = values_in - row_mean
    row_var = lax.optimization_barrier(jnp.mean(centred * centred, axis=-1, keepdims=True))
    return centred * lax.rsqrt(row_var + EPSILON) * gain_vec + shift_vec

def ancestor_table(parent_row):
    seg_index = jnp.arange(SEGS, dtype=jnp.int32)
    grand_row = jnp.where(parent_row >= 0, parent_row[jnp.maximum(parent_row, 0)], -1)
    own_seg = seg_index[:, None] == seg_index[None, :]
    parent_hit = parent_row[:, None] == seg_index[None, :]
    grand_hit = grand_row[:, None] == seg_index[None, :]
    return own_seg | parent_hit | grand_hit

def tree_mask(parent_row, start_row, length_row):
    places = jnp.arange(TREE_TOK, dtype=jnp.int32)
    inside = (places[:, None] >= start_row[None, :]) & (places[:, None] < (start_row + length_row)[None, :])
    seg_ids = lax.optimization_barrier(jnp.sum(jnp.where(inside, jnp.arange(SEGS, dtype=jnp.int32)[None, :], 0), axis=1)).astype(jnp.int32)
    table = ancestor_table(parent_row)
    visible = table[seg_ids][:, seg_ids]
    same_seg = seg_ids[:, None] == seg_ids[None, :]
    causal = places[None, :] <= places[:, None]
    return visible & (jnp.logical_not(same_seg) | causal)

def head_attend(query_head, keys_part, values_part, visible):
    score_scale = HD ** (-0.5)
    scores = low_back(matmul(query_head, keys_part.T) * score_scale)
    masked = jnp.where(visible, scores, -1e+30)
    row_top = lax.optimization_barrier(jnp.max(masked, axis=1, keepdims=True))
    exp_scores = jnp.exp(masked - row_top)
    weights = exp_scores / lax.optimization_barrier(jnp.sum(exp_scores, axis=1, keepdims=True))
    return matmul(low(weights), values_part)

def tree_attend(pieces):
    tree_queries, tree_keyval, parent_row, start_row, length_row = pieces
    visible = tree_mask(parent_row, start_row, length_row)
    keys_part = tree_keyval[:, :HD]
    values_part = tree_keyval[:, HD:]

    def one_head(query_head):
        return head_attend(query_head, keys_part, values_part, visible)
    return lax.map(jax.checkpoint(one_head), tree_queries)

def forward(params, seg_parent, seg_start, seg_length):
    block_in, attn_gain, attn_shift, query_weight, query_bias, keyval_weight, value_bias, output_weight, output_bias, mlp_gain, mlp_shift, expand_weight, expand_bias, shrink_weight, shrink_bias = params
    normed = low(layer_norm(block_in, attn_gain, attn_shift))
    queries = low(low_back(matmul(normed, query_weight) + query_bias))
    value_shift = jnp.concatenate([jnp.zeros((HD,), jnp.float32), value_bias])
    keyval = low(low_back(matmul(normed, keyval_weight) + value_shift))
    tree_queries = queries.reshape(TREES, TREE_TOK, H, HD).transpose(0, 2, 1, 3)
    tree_keyval = keyval.reshape(TREES, TREE_TOK, 2 * HD)
    attended = lax.map(jax.checkpoint(tree_attend), (tree_queries, tree_keyval, seg_parent, seg_start, seg_length))
    attended = attended.transpose(0, 2, 1, 3).reshape(TOKENS, D)
    attended = low(low_back(attended))
    middle = block_in + low_back(matmul(attended, output_weight) + output_bias)
    normed_two = low(layer_norm(middle, mlp_gain, mlp_shift))
    pre_act = low_back(matmul(normed_two, expand_weight) + expand_bias)
    activ = low(jax.nn.gelu(pre_act, approximate=True))
    return middle + low_back(matmul(activ, shrink_weight) + shrink_bias)

def reference(block_input, cotangent, attn_gain, attn_shift, query_weight, query_bias, keyval_weight, value_bias, output_weight, output_bias, mlp_gain, mlp_shift, expand_weight, expand_bias, shrink_weight, shrink_bias, seg_parent, seg_start, seg_length):
    floats = tuple((array.astype(jnp.float32) for array in (block_input, attn_gain, attn_shift, query_weight, query_bias, keyval_weight, value_bias, output_weight, output_bias, mlp_gain, mlp_shift, expand_weight, expand_bias, shrink_weight, shrink_bias)))

    def wrapped(*params):
        return forward(params, seg_parent, seg_start, seg_length)
    result, pullback = jax.vjp(wrapped, *floats)
    grads = pullback(cotangent.astype(jnp.float32))
    return (result.astype(jnp.bfloat16), grads[0], grads[1], grads[2], grads[3], grads[4], grads[5], grads[6], grads[7], grads[8], grads[9], grads[10], grads[11], grads[12], grads[13], grads[14])
```

```python
import functools
import math

import jax
import jax.numpy as jnp
from jax import lax
from jax.experimental import pallas as pl
from jax.experimental.pallas import tpu as pltpu
from jax.sharding import PartitionSpec as P

HD = 128
TREE_TOK = 5120
TRUNK = 2048
EPSILON = 1e-05
SCALE = HD**-0.5
SCALE2 = SCALE * math.log2(math.e)
NEG = -1e30
TILE = 512
BF = jnp.bfloat16
F32 = jnp.float32
VMEM_BYTES = 60 * 1024 * 1024


def dot(a, b, out=F32):
    return jnp.dot(a, b, preferred_element_type=F32).astype(out)


def dot_t(a, b, out=F32):
    return lax.dot_general(a, b, (((1,), (1,)), ((), ())), preferred_element_type=F32).astype(out)


def dot_0(a, b, out=F32):
    return lax.dot_general(a, b, (((0,), (0,)), ((), ())), preferred_element_type=F32).astype(out)


def tail_rows(tab, i):
    return pl.ds(pl.multiple_of(tab[2, i], 128), TILE // 2), pl.ds(
        pl.multiple_of(tab[4, i], 128), TILE // 2
    )


def fwd_kernel(tab, q_ref, k_ref, v_ref, o_ref, lse_ref, *, bs, heads, hg):
    i = pl.program_id(0)
    full, base = tab[0, i], tab[1, i]
    lim0, lim1 = tab[3, i], tab[5, i]
    half = TILE // 2
    r0, r1 = tail_rows(tab, i)
    row = lax.broadcasted_iota(jnp.int32, (hg * bs, TILE), 0) & (bs - 1)
    col = lax.broadcasted_iota(jnp.int32, (hg * bs, TILE), 1)
    mask = col <= row + jnp.where(col < half, lim0, lim1 + half)
    for g in range(heads // hg):
        cols = [slice((g * hg + h) * HD, (g * hg + h + 1) * HD) for h in range(hg)]
        q = jnp.concatenate([q_ref[:, c] for c in cols], axis=0)
        kt = jnp.concatenate([k_ref[r0, :], k_ref[r1, :]], axis=0)
        vt = jnp.concatenate([v_ref[r0, :], v_ref[r1, :]], axis=0)
        s = jnp.where(mask, dot_t(q, kt) * SCALE2, NEG)
        top = jnp.max(s, axis=1, keepdims=True)
        acc = dot(jnp.exp2(s - top).astype(BF), vt)

        def body(t, carry):
            top, acc = carry
            rr = pl.ds(pl.multiple_of(base + t * TILE, 128), TILE)
            s = dot_t(q, k_ref[rr, :]) * SCALE2
            new = jnp.maximum(top, jnp.max(s, axis=1, keepdims=True))
            p = jnp.exp2(s - new).astype(BF)
            return new, acc * jnp.exp2(top - new) + dot(p, v_ref[rr, :])

        top, acc = lax.fori_loop(0, full, body, (top, acc))
        total = acc[:, HD:]
        out = (acc[:, :HD] / total).astype(BF)
        lse = top + jnp.log2(total)
        for h in range(hg):
            o_ref[:, cols[h]] = out[h * bs : (h + 1) * bs]
            lse_ref[0, g * hg + h : g * hg + h + 1, :] = jnp.transpose(lse[h * bs : (h + 1) * bs])[0:1, :]


def attention_forward(tab, q, k, v_ext, blocks):
    tokens, width = q.shape
    bs, heads = tokens // blocks, width // HD
    return pl.pallas_call(
        functools.partial(fwd_kernel, bs=bs, heads=heads, hg=heads),
        grid_spec=pltpu.PrefetchScalarGridSpec(
            num_scalar_prefetch=1,
            grid=(blocks,),
            in_specs=[
                pl.BlockSpec((bs, width), lambda i, t: (i, 0)),
                pl.BlockSpec(k.shape, lambda i, t: (0, 0)),
                pl.BlockSpec(v_ext.shape, lambda i, t: (0, 0)),
            ],
            out_specs=[
                pl.BlockSpec((bs, width), lambda i, t: (i, 0)),
                pl.BlockSpec((1, heads, bs), lambda i, t: (i, 0, 0)),
            ],
        ),
        out_shape=[
            jax.ShapeDtypeStruct((tokens, width), BF),
            jax.ShapeDtypeStruct((blocks, heads, bs), F32),
        ],
        compiler_params=pltpu.CompilerParams(vmem_limit_bytes=VMEM_BYTES),
        cost_estimate=pl.CostEstimate(
            flops=int(4 * tokens * heads * 2304 * 2 * HD), bytes_accessed=10_000_000, transcendentals=tokens * heads * 2304
        ),
        name="attn_fwd",
    )(tab, q, k, v_ext)


def bwd_kernel(tab, q_ref, da_ref, a_ref, lse_ref, k_ref, v_ref, dq_ref, dkv_ref, *, bs, heads, hg):
    i = pl.program_id(0)
    full, base = tab[0, i], tab[1, i]
    lim0, lim1 = tab[3, i], tab[5, i]
    half = TILE // 2
    r0, r1 = tail_rows(tab, i)
    row = lax.broadcasted_iota(jnp.int32, (TILE, hg * bs), 1) & (bs - 1)
    col = lax.broadcasted_iota(jnp.int32, (TILE, hg * bs), 0)
    mask = col <= row + jnp.where(col < half, lim0, lim1 + half)

    @pl.when(i == 0)
    def _():
        dkv_ref[...] = jnp.zeros_like(dkv_ref)

    for g in range(heads // hg):
        cols = [slice((g * hg + h) * HD, (g * hg + h + 1) * HD) for h in range(hg)]
        q = jnp.concatenate([q_ref[:, c] for c in cols], axis=0)
        da = jnp.concatenate([da_ref[:, c] for c in cols], axis=0)
        lse = jnp.concatenate([lse_ref[0, g * hg + h : g * hg + h + 1, :] for h in range(hg)], axis=1)
        delta = jnp.concatenate(
            [
                jnp.sum(
                    jnp.transpose(da_ref[:, c].astype(F32) * a_ref[:, c].astype(F32)), axis=0, keepdims=True
                )
                for c in cols
            ],
            axis=1,
        )

        def tile(kt, vt, visible):
            st = dot_t(kt, q) * SCALE2 - lse
            if visible is not None:
                st = jnp.where(visible, st, NEG)
            pt = jnp.exp2(st)
            dst = (pt * (dot_t(vt, da) - delta)).astype(BF)
            return dot(dst, q) * SCALE, dot(pt.astype(BF), da), dot_0(dst, kt)

        kt = jnp.concatenate([k_ref[r0, :], k_ref[r1, :]], axis=0)
        vt = jnp.concatenate([v_ref[r0, :], v_ref[r1, :]], axis=0)
        dk, dv, dq = tile(kt, vt, mask)
        dkv_ref[r0, :HD] += dk[:half]
        dkv_ref[r0, HD:] += dv[:half]
        dkv_ref[r1, :HD] += dk[half:]
        dkv_ref[r1, HD:] += dv[half:]

        def body(t, dq):
            rr = pl.ds(pl.multiple_of(base + t * TILE, 128), TILE)
            dk, dv, more = tile(k_ref[rr, :], v_ref[rr, :], None)
            dkv_ref[rr, :HD] += dk
            dkv_ref[rr, HD:] += dv
            return dq + more

        dq = (lax.fori_loop(0, full, body, dq) * SCALE).astype(BF)
        for h in range(hg):
            dq_ref[:, cols[h]] = dq[h * bs : (h + 1) * bs]


def attention_backward(tab, q, da, a, lse, k, v, blocks):
    tokens, width = q.shape
    bs, heads = tokens // blocks, width // HD
    qs = pl.BlockSpec((bs, width), lambda i, t: (i, 0))
    ks = pl.BlockSpec(k.shape, lambda i, t: (0, 0))
    return pl.pallas_call(
        functools.partial(bwd_kernel, bs=bs, heads=heads, hg=heads),
        grid_spec=pltpu.PrefetchScalarGridSpec(
            num_scalar_prefetch=1,
            grid=(blocks,),
            in_specs=[qs, qs, qs, pl.BlockSpec((1, heads, bs), lambda i, t: (i, 0, 0)), ks, ks],
            out_specs=[qs, pl.BlockSpec((k.shape[0], 2 * HD), lambda i, t: (0, 0))],
        ),
        out_shape=[
            jax.ShapeDtypeStruct((tokens, width), BF),
            jax.ShapeDtypeStruct((k.shape[0], 2 * HD), F32),
        ],
        compiler_params=pltpu.CompilerParams(vmem_limit_bytes=VMEM_BYTES),
        cost_estimate=pl.CostEstimate(
            flops=int(10 * tokens * heads * 2304 * 2 * HD), bytes_accessed=20_000_000, transcendentals=tokens * heads * 2304
        ),
        name="attn_bwd",
    )(tab, q, da, a, lse, k, v)


def block_table(parent, start, places):
    slots = jnp.arange(parent.shape[0], dtype=jnp.int32)
    length = jnp.where(parent < 0, TRUNK, TILE // 2)
    mine = (places[:, None] >= start[None, :]) & (places[:, None] < (start + length)[None, :])
    pick = lambda sel, vals: jnp.sum(jnp.where(sel, vals[None, :], 0), axis=1)
    seg = pick(mine, slots)
    own = pick(mine, start)
    par = pick(mine, parent)
    is_par = slots[None, :] == par[:, None]
    par_start = pick(is_par, start)
    grand = jnp.where(par < 0, -1, pick(is_par, parent))
    trunk = jnp.sum(jnp.where(parent < 0, start, 0))
    off = places - own
    in_trunk, leaf = par < 0, grand >= 0
    full = jnp.where(in_trunk, off // TILE, TRUNK // TILE)
    half = TILE // 2
    first = jnp.where(in_trunk, trunk + full * TILE, jnp.where(leaf, par_start, own))
    lim_first = jnp.where(in_trunk, off - full * TILE, jnp.where(leaf, 2 * TILE, off))
    second = jnp.where(in_trunk, trunk + full * TILE + half, own)
    lim_second = jnp.where(in_trunk, off - full * TILE - half, jnp.where(leaf, off, -2 * TILE))
    return jnp.stack([full, jnp.full_like(full, trunk), first, lim_first, second, lim_second]).astype(jnp.int32)


def normalise(x):
    mean = jnp.mean(x, axis=1, keepdims=True)
    cent = x - mean
    inv = lax.rsqrt(jnp.mean(cent * cent, axis=1, keepdims=True) + EPSILON)
    return mean, inv


def norm_back(grad, xhat, inv, gain):
    c = grad * gain
    return inv * (c - jnp.mean(c, axis=1, keepdims=True) - xhat * jnp.mean(c * xhat, axis=1, keepdims=True))


def gelu_both(u):
    k, a = math.sqrt(2 / math.pi), 0.044715
    t = jnp.tanh(k * (u + a * u * u * u))
    return 0.5 * u * (1 + t), 0.5 * (1 + t) + 0.5 * u * (1 - t * t) * (k * (1 + 3 * a * u * u))


def on_device(
    block_input,
    cotangent,
    attn_gain,
    attn_shift,
    query_weight,
    query_bias,
    keyval_weight,
    value_bias,
    output_weight,
    output_bias,
    mlp_gain,
    mlp_shift,
    expand_weight,
    expand_bias,
    shrink_weight,
    shrink_bias,
    seg_parent,
    seg_start,
    seg_length,
):
    rows, cols = lax.axis_size("row"), lax.axis_size("col")
    core, me, z = lax.axis_index("dp"), lax.axis_index("row"), lax.axis_index("col")
    local, feat = block_input.shape
    width = feat * rows
    tokens = local // rows
    bs = math.gcd(tokens, 128)
    blocks = tokens // bs
    ev = query_weight.shape[1]
    ff = expand_weight.shape[1]
    eh, fh = ev // 2, ff // 2
    swap = lambda x: lax.ppermute(x, "dp", [(0, 1), (1, 0)])
    z_one = lambda x: lax.ppermute(x, "col", [(i, i ^ 1) for i in range(cols)])
    z_two = lambda x: lax.ppermute(x, "col", [(i, i ^ 2) for i in range(cols)])

    def to_rows(x):
        x = x.reshape(blocks, rows, bs, feat).transpose(1, 0, 2, 3).reshape(local, feat)
        return lax.all_to_all(x, "row", split_axis=0, concat_axis=1, tiled=True)

    def from_rows(x):
        x = lax.all_to_all(x, "row", split_axis=1, concat_axis=0, tiled=True)
        return x.reshape(rows, blocks, bs, feat).transpose(1, 0, 2, 3).reshape(local, feat)

    def by_core(own, other, axis):
        return jnp.where(
            core == 0, jnp.concatenate([own, other], axis), jnp.concatenate([other, own], axis)
        )

    vectors = jnp.stack([attn_gain, attn_shift, output_bias, mlp_gain, mlp_shift, shrink_bias])
    vectors = lax.all_gather(vectors, "row", axis=1, tiled=True).astype(F32)
    gain_one, shift_one, out_bias, gain_two, shift_two, down_bias = (vectors[i : i + 1] for i in range(6))
    q_bias = lax.all_gather(query_bias, "col", axis=0, tiled=True).astype(F32).reshape(cols, 2, eh)
    half_of = lambda x, c, size, axis: lax.dynamic_slice_in_dim(x, c * size, size, axis)
    q_bias = jnp.concatenate(
        [lax.dynamic_index_in_dim(q_bias, c, 1, False).reshape(1, cols * eh) for c in (core, 1 - core)], axis=1
    )
    up_bias = half_of(expand_bias, core, fh, 0)
    up_bias = [up_bias.astype(F32)[None], z_two(up_bias).astype(F32)[None]]

    x = to_rows(block_input).astype(F32)
    kv_weight = lax.all_gather(keyval_weight, "row", axis=0, tiled=True)

    def gather_square(block):
        own = lax.all_gather(block, ("row", "col"), axis=0, tiled=False)
        own = own.reshape(rows, cols, feat, eh).transpose(0, 2, 1, 3).reshape(width, cols * eh)
        return jnp.concatenate([own, swap(own)], axis=1)

    wq = gather_square(half_of(query_weight, core, eh, 1))
    wo_t = gather_square(half_of(output_weight, core, eh, 0).T)

    mean_one, inv_one = normalise(x)
    normed = ((x - mean_one) * inv_one * gain_one + shift_one).astype(BF)
    kv_shift = jnp.concatenate([jnp.zeros((HD,), F32), value_bias.astype(F32)])[None]
    kv = (dot(normed, kv_weight) + kv_shift).astype(BF)
    kv_other = z_one(kv)
    odd = z % 2
    kv_pair = jnp.where(odd == 0, jnp.stack([kv, kv_other]), jnp.stack([kv_other, kv]))
    kv_all = lax.all_gather(kv_pair, "row", axis=0, tiled=False)
    kv_all = kv_all.reshape(rows, 2, blocks, bs, 2 * HD).transpose(1, 2, 0, 3, 4).reshape(2 * local, 2 * HD)
    keys, values = kv_all[:, :HD], kv_all[:, HD:]
    q = (dot(normed, wq) + q_bias).astype(BF)

    up = half_of(expand_weight, core, fh, 1)
    down_t = half_of(shrink_weight, core, fh, 0).T
    gather_rows = lambda w: lax.all_gather(w, "row", axis=0, tiled=True)
    up_w = [gather_rows(up), gather_rows(z_two(up))]
    down_w = [gather_rows(down_t), gather_rows(z_two(down_t))]

    dy = to_rows(cotangent)

    def quad(x):
        far = z_one(x)
        return jnp.concatenate([x, swap(x)]), jnp.concatenate([far, swap(far)])

    dy_all = quad(dy)

    tree = z // 2
    tree_row = lambda t: lax.dynamic_index_in_dim(t, tree, 0, False)
    places = odd * local + (jnp.arange(blocks, dtype=jnp.int32) * rows + me) * bs
    tab = block_table(tree_row(seg_parent), tree_row(seg_start), places)
    v_ext = jnp.concatenate([values, jnp.ones_like(values)], axis=1)
    att, lse = attention_forward(tab, q, keys, v_ext, blocks)
    mid = x + dot_t(att, wo_t) + out_bias

    mean_two, inv_two = normalise(mid)
    xhat_two = (mid - mean_two) * inv_two
    normed_two = (xhat_two * gain_two + shift_two).astype(BF)
    n2 = quad(normed_two)
    act, slope = [[None] * 2, [None] * 2], [[None] * 2, [None] * 2]
    for a in range(2):
        for c in range(2):
            g, s = gelu_both(dot(n2[a], up_w[c]) + up_bias[c])
            act[a][c], slope[a][c] = g.astype(BF), s.astype(BF)

    def reduce_quad(near, far):
        far_got = swap(far[tokens:].astype(BF))
        far_sum = z_one((far[:tokens] + far_got.astype(F32)).astype(BF))
        near_got = swap(near[tokens:].astype(BF))
        return near[:tokens] + near_got.astype(F32) + far_sum.astype(F32)

    dpre = [[None] * 2, [None] * 2]
    for a in range(2):
        for c in range(2):
            dpre[a][c] = (dot(dy_all[a], down_w[c]) * slope[a][c].astype(F32)).astype(BF)
    dn2 = reduce_quad(*[dot_t(dpre[a][0], up_w[0]) + dot_t(dpre[a][1], up_w[1]) for a in (0, 1)])

    branch = reduce_quad(*[dot_t(act[a][0], down_w[0]) + dot_t(act[a][1], down_w[1]) for a in (0, 1)])
    block_output = from_rows((mid + branch + down_bias).astype(BF))

    scatter_rows = lambda w: lax.psum_scatter(w, "row", scatter_dimension=0, tiled=True)

    def hidden_grads(left, right):
        part = [
            scatter_rows((dot_0(left[0], right[0][c]) + dot_0(left[1], right[1][c])).astype(BF)) for c in (1, 0)
        ]
        return (part[1].astype(F32) + z_two(part[0]).astype(F32)).astype(BF)

    d_down = hidden_grads(dy_all, act)
    d_up = hidden_grads(n2, dpre)
    expand_weight_grad = by_core(d_up, swap(d_up), 1).astype(F32)
    shrink_weight_grad = by_core(d_down.T, swap(d_down.T), 0).astype(F32)

    dmid = dy.astype(F32) + norm_back(dn2, xhat_two, inv_two, gain_two)
    dmid_low = dmid.astype(BF)
    datt = dot(dmid_low, wo_t, BF)
    dq, dkv_part = attention_backward(tab, q, datt, att, lse, keys, values, blocks)

    def square_grad(left, right):
        mine, other = right[:, : cols * eh], right[:, cols * eh :]
        got = swap(dot_0(left, other, BF))
        full = scatter_rows((dot_0(left, mine) + got.astype(F32)).astype(BF))
        full = full.reshape(feat, cols, eh).transpose(1, 0, 2)
        return lax.psum_scatter(full, "col", scatter_dimension=0, tiled=False)

    d_out = square_grad(dmid_low, att)
    output_weight_grad = by_core(d_out.T, swap(d_out.T), 0).astype(F32)
    dkv_half = dkv_part.reshape(2, local, 2 * HD).astype(BF)
    dkv_got = z_one(lax.dynamic_index_in_dim(dkv_half, 1 - odd, 0, False))
    dkv_sum = half_of(dkv_part, odd, local, 0) + dkv_got.astype(F32)
    dkv_sum = dkv_sum.astype(BF).reshape(blocks, rows, bs, 2 * HD).transpose(1, 0, 2, 3).reshape(local, 2 * HD)
    dkv = scatter_rows(dkv_sum)
    d_query = square_grad(normed, dq)
    query_weight_grad = by_core(d_query, swap(d_query), 1).astype(F32)

    dn1 = dot_t(dq, wq) + dot_t(dkv, kv_weight)
    xhat_one = (x - mean_one) * inv_one
    input_grad = from_rows((dmid + norm_back(dn1, xhat_one, inv_one, gain_one)).astype(BF)).astype(F32)
    d_kv_weight = scatter_rows(dot_0(normed, dkv, BF))
    keyval_weight_grad = lax.psum(d_kv_weight, ("dp", "col")).astype(F32)

    everyone = ("dp", "row", "col")
    total = lambda t: jnp.sum(t.astype(F32), axis=0)
    bias_up = jnp.zeros((cols, 2, fh), F32)
    for c, where in ((0, z), (1, z ^ 2)):
        bias_up = lax.dynamic_update_slice(
            bias_up, (total(dpre[0][c]) + total(dpre[1][c]))[None, None], (where, core, 0)
        )
    early = jnp.concatenate(
        [total(dn2 * xhat_two), total(dn2), total(dmid_low), total(dy), bias_up.reshape(-1)]
    )
    early = lax.psum(early, everyone)
    dq_sum = total(dq).reshape(2, cols, eh)
    dq_sum = jnp.where(core == 0, dq_sum, dq_sum[::-1]).transpose(1, 0, 2).reshape(-1)
    late = jnp.concatenate([total(dn1 * xhat_one), total(dn1), dq_sum, total(dkv[:, HD:])])
    late = lax.psum(late, everyone)
    row_part = lambda v, n: half_of(v[n * width : (n + 1) * width], me, feat, 0)
    return (
        block_output,
        input_grad,
        row_part(late, 0),
        row_part(late, 1),
        query_weight_grad,
        half_of(late[2 * width : 3 * width], z, ev, 0),
        keyval_weight_grad,
        late[3 * width :],
        output_weight_grad,
        row_part(early, 2),
        row_part(early, 0),
        row_part(early, 1),
        expand_weight_grad,
        half_of(early[4 * width :], z, ff, 0),
        shrink_weight_grad,
        row_part(early, 3),
    )


def solution(mesh):
    tokens, row, col = P(("dp", "col"), "row"), P("row"), P("col")
    tree = P("dp", None)
    return jax.shard_map(
        on_device,
        mesh=mesh,
        in_specs=(
            tokens, tokens, row, row, P("row", "col"), col, P("row", None), P(), P("col", "row"), row,
            row, row, P("row", "col"), col, P("col", "row"), row, tree, tree, tree,
        ),
        out_specs=(
            tokens, tokens, row, row, P("row", "col"), col, P("row", None), P(), P("col", "row"), row,
            row, row, P("row", "col"), col, P("col", "row"), row,
        ),
        check_vma=False,
    )
```

```python
import functools
import math

import jax
import jax.numpy as jnp
from jax import lax
from jax.experimental import pallas as pl
from jax.experimental.pallas import tpu as pltpu
from jax.sharding import PartitionSpec as P

HD = 128
TREE_TOK = 5120
TRUNK = 2048
EPSILON = 1e-05
SCALE = HD**-0.5
SCALE2 = SCALE * math.log2(math.e)
NEG = -1e30
TILE = 512
BF = jnp.bfloat16
F32 = jnp.float32
VMEM_BYTES = 60 * 1024 * 1024


def dot(a, b, out=F32):
    return jnp.dot(a, b, preferred_element_type=F32).astype(out)


def dot_t(a, b, out=F32):
    return lax.dot_general(a, b, (((1,), (1,)), ((), ())), preferred_element_type=F32).astype(out)


def dot_0(a, b, out=F32):
    return lax.dot_general(a, b, (((0,), (0,)), ((), ())), preferred_element_type=F32).astype(out)


def tail_rows(tab, i):
    return pl.ds(pl.multiple_of(tab[2, i], 128), TILE // 2), pl.ds(
        pl.multiple_of(tab[4, i], 128), TILE // 2
    )


def place_of(head, heads):
    half = heads // 2
    return head // half, slice(head % half * HD, (head % half + 1) * HD)


def fwd_kernel(tab, *refs, bs, heads, hg):
    qa_ref, qb_ref, k_ref, v_ref = refs[:4]
    oa_ref, ob_ref, lse_ref = refs[-3:]
    i = pl.program_id(0)
    full, base = tab[0, i], tab[1, i]
    lim0, lim1 = tab[3, i], tab[5, i]
    half = TILE // 2
    r0, r1 = tail_rows(tab, i)
    row = lax.broadcasted_iota(jnp.int32, (hg * bs, TILE), 0) & (bs - 1)
    col = lax.broadcasted_iota(jnp.int32, (hg * bs, TILE), 1)
    mask = col <= row + jnp.where(col < half, lim0, lim1 + half)
    for g in range(heads // hg):
        at = [place_of(g * hg + h, heads) for h in range(hg)]
        q = jnp.concatenate([(qa_ref, qb_ref)[w][:, c] for w, c in at], axis=0)
        kt = jnp.concatenate([k_ref[r0, :], k_ref[r1, :]], axis=0)
        vt = jnp.concatenate([v_ref[r0, :], v_ref[r1, :]], axis=0)
        s = jnp.where(mask, dot_t(q, kt) * SCALE2, NEG)
        top = jnp.max(s, axis=1, keepdims=True)
        acc = dot(jnp.exp2(s - top).astype(BF), vt)

        def body(t, carry):
            top, acc = carry
            rr = pl.ds(pl.multiple_of(base + t * TILE, 128), TILE)
            s = dot_t(q, k_ref[rr, :]) * SCALE2
            new = jnp.maximum(top, jnp.max(s, axis=1, keepdims=True))
            p = jnp.exp2(s - new).astype(BF)
            return new, acc * jnp.exp2(top - new) + dot(p, v_ref[rr, :])

        top, acc = lax.fori_loop(0, full, body, (top, acc))
        total = acc[:, HD:]
        out = (acc[:, :HD] / total).astype(BF)
        lse = top + jnp.log2(total)
        for h in range(hg):
            (oa_ref, ob_ref)[at[h][0]][:, at[h][1]] = out[h * bs : (h + 1) * bs]
            lse_ref[0, g * hg + h : g * hg + h + 1, :] = jnp.transpose(lse[h * bs : (h + 1) * bs])[0:1, :]


def attention_forward(tab, q, k, v_ext, blocks, *needs):
    tokens, width = q[0].shape
    bs, heads = tokens // blocks, 2 * width // HD
    qs = pl.BlockSpec((bs, width), lambda i, t: (i, 0))
    return pl.pallas_call(
        functools.partial(fwd_kernel, bs=bs, heads=heads, hg=heads),
        grid_spec=pltpu.PrefetchScalarGridSpec(
            num_scalar_prefetch=1,
            grid=(blocks,),
            in_specs=[
                qs,
                qs,
                pl.BlockSpec(k.shape, lambda i, t: (0, 0)),
                pl.BlockSpec(v_ext.shape, lambda i, t: (0, 0)),
            ]
            + [ANY] * len(needs),
            out_specs=[
                qs,
                qs,
                pl.BlockSpec((1, heads, bs), lambda i, t: (i, 0, 0)),
            ],
        ),
        out_shape=[
            jax.ShapeDtypeStruct((tokens, width), BF),
            jax.ShapeDtypeStruct((tokens, width), BF),
            jax.ShapeDtypeStruct((blocks, heads, bs), F32),
        ],
        compiler_params=pltpu.CompilerParams(vmem_limit_bytes=VMEM_BYTES),
        cost_estimate=SMALL,
        name="attn_fwd",
    )(tab, *q, k, v_ext, *needs)


def bwd_kernel(tab, *refs, bs, heads, hg, more):
    qa_ref, qb_ref, daa_ref, dab_ref, aa_ref, ab_ref, lse_ref, k_ref, v_ref = refs[:9]
    dqa_ref, dqb_ref, dkv_ref = refs[-3:]
    i = pl.program_id(0)
    full, base = tab[0, i], tab[1, i]
    lim0, lim1 = tab[3, i], tab[5, i]
    half = TILE // 2
    r0, r1 = tail_rows(tab, i)
    row = lax.broadcasted_iota(jnp.int32, (TILE, hg * bs), 1) & (bs - 1)
    col = lax.broadcasted_iota(jnp.int32, (TILE, hg * bs), 0)
    mask = col <= row + jnp.where(col < half, lim0, lim1 + half)

    @pl.when(i == 0)
    def _():
        dkv_ref[...] = refs[9][...] if more else jnp.zeros_like(dkv_ref)

    for g in range(heads // hg):
        at = [place_of(g * hg + h, heads) for h in range(hg)]
        q = jnp.concatenate([(qa_ref, qb_ref)[w][:, c] for w, c in at], axis=0)
        da = jnp.concatenate([(daa_ref, dab_ref)[w][:, c] for w, c in at], axis=0)
        lse = jnp.concatenate([lse_ref[0, g * hg + h : g * hg + h + 1, :] for h in range(hg)], axis=1)
        delta = jnp.concatenate(
            [
                jnp.sum(
                    jnp.transpose((daa_ref, dab_ref)[w][:, c].astype(F32) * (aa_ref, ab_ref)[w][:, c].astype(F32)),
                    axis=0,
                    keepdims=True,
                )
                for w, c in at
            ],
            axis=1,
        )

        def tile(kt, vt, visible):
            st = dot_t(kt, q) * SCALE2 - lse
            if visible is not None:
                st = jnp.where(visible, st, NEG)
            pt = jnp.exp2(st)
            dst = (pt * (dot_t(vt, da) - delta)).astype(BF)
            return dot(dst, q) * SCALE, dot(pt.astype(BF), da), dot_0(dst, kt)

        kt = jnp.concatenate([k_ref[r0, :], k_ref[r1, :]], axis=0)
        vt = jnp.concatenate([v_ref[r0, :], v_ref[r1, :]], axis=0)
        dk, dv, dq = tile(kt, vt, mask)
        dkv_ref[r0, :HD] += dk[:half]
        dkv_ref[r0, HD:] += dv[:half]
        dkv_ref[r1, :HD] += dk[half:]
        dkv_ref[r1, HD:] += dv[half:]

        def body(t, dq):
            rr = pl.ds(pl.multiple_of(base + t * TILE, 128), TILE)
            dk, dv, more = tile(k_ref[rr, :], v_ref[rr, :], None)
            dkv_ref[rr, :HD] += dk
            dkv_ref[rr, HD:] += dv
            return dq + more

        dq = (lax.fori_loop(0, full, body, dq) * SCALE).astype(BF)
        for h in range(hg):
            (dqa_ref, dqb_ref)[at[h][0]][:, at[h][1]] = dq[h * bs : (h + 1) * bs]


def attention_backward(tab, q, da, a, lse, k, v, blocks, first, count, so_far, *needs):
    tokens, width = q[0].shape
    bs, heads = tokens // blocks, 2 * width // HD
    qs = pl.BlockSpec((bs, width), lambda i, t: (i + first, 0))
    ks = pl.BlockSpec(k.shape, lambda i, t: (0, 0))
    whole = pl.BlockSpec((k.shape[0], 2 * HD), lambda i, t: (0, 0))
    out = pl.BlockSpec((bs, width), lambda i, t: (i, 0))
    more = [] if so_far is None else [so_far]
    return pl.pallas_call(
        functools.partial(bwd_kernel, bs=bs, heads=heads, hg=heads, more=bool(more)),
        grid_spec=pltpu.PrefetchScalarGridSpec(
            num_scalar_prefetch=1,
            grid=(count,),
            in_specs=[qs] * 6
            + [pl.BlockSpec((1, heads, bs), lambda i, t: (i + first, 0, 0)), ks, ks]
            + [whole] * len(more)
            + [ANY] * len(needs),
            out_specs=[out, out, whole],
        ),
        out_shape=[
            jax.ShapeDtypeStruct((count * bs, width), BF),
            jax.ShapeDtypeStruct((count * bs, width), BF),
            jax.ShapeDtypeStruct((k.shape[0], 2 * HD), F32),
        ],
        compiler_params=pltpu.CompilerParams(vmem_limit_bytes=VMEM_BYTES),
        cost_estimate=SMALL,
        name="attn_bwd",
    )(tab[:, first : first + count], *q, *da, *a, lse, k, v, *more, *needs)


def block_table(parent, start, places):
    slots = jnp.arange(parent.shape[0], dtype=jnp.int32)
    length = jnp.where(parent < 0, TRUNK, TILE // 2)
    mine = (places[:, None] >= start[None, :]) & (places[:, None] < (start + length)[None, :])
    pick = lambda sel, vals: jnp.sum(jnp.where(sel, vals[None, :], 0), axis=1)
    seg = pick(mine, slots)
    own = pick(mine, start)
    par = pick(mine, parent)
    is_par = slots[None, :] == par[:, None]
    par_start = pick(is_par, start)
    grand = jnp.where(par < 0, -1, pick(is_par, parent))
    trunk = jnp.sum(jnp.where(parent < 0, start, 0))
    off = places - own
    in_trunk, leaf = par < 0, grand >= 0
    full = jnp.where(in_trunk, off // TILE, TRUNK // TILE)
    half = TILE // 2
    first = jnp.where(in_trunk, trunk + full * TILE, jnp.where(leaf, par_start, own))
    lim_first = jnp.where(in_trunk, off - full * TILE, jnp.where(leaf, 2 * TILE, off))
    second = jnp.where(in_trunk, trunk + full * TILE + half, own)
    lim_second = jnp.where(in_trunk, off - full * TILE - half, jnp.where(leaf, off, -2 * TILE))
    return jnp.stack([full, jnp.full_like(full, trunk), first, lim_first, second, lim_second]).astype(jnp.int32)


SMALL = pl.CostEstimate(flops=1_000_000, bytes_accessed=1_000_000, transcendentals=0)
ANY = pl.BlockSpec(memory_space=pl.ANY)


def hold(values, *needs):
    values = list(values)
    n, m = len(values), len(needs)
    out = pl.pallas_call(
        lambda *refs: None,
        in_specs=[ANY] * (n + m),
        out_specs=[ANY] * n,
        out_shape=[jax.ShapeDtypeStruct(v.shape, v.dtype) for v in values],
        input_output_aliases={i: i for i in range(n)},
        cost_estimate=SMALL,
        name="hold",
    )(*values, *needs)
    return list(out)


def up_kernel(*refs, half, step):
    xa, xb, ya, yb, w, b = refs[:6]
    g_ref, du_ref = refs[-2:]

    def go(x, y):
        for j in range(0, w.shape[2], step):
            c = slice(j, j + step)
            u = dot(x[...], w[0, :, c]) + b[:, c]
            d = dot(y[...], w[1, :, c])
            g, slope = gelu_both(u)
            g_ref[:, c] = g.astype(BF)
            du_ref[:, c] = (d * slope).astype(BF)

    pl.when(pl.program_id(0) < half)(lambda: go(xa, ya))
    pl.when(pl.program_id(0) >= half)(lambda: go(xb, yb))


def up(x, dy, w, b, *needs):
    tokens, width = x[0].shape
    hidden = w.shape[2]
    tm, half = tokens // 2, 2
    first = pl.BlockSpec((tm, width), lambda i: (jnp.minimum(i, half - 1), 0))
    second = pl.BlockSpec((tm, width), lambda i: (jnp.maximum(i - half, 0), 0))
    return pl.pallas_call(
        functools.partial(up_kernel, half=half, step=512),
        grid=(2 * half,),
        in_specs=[first, second, first, second, pl.BlockSpec(w.shape, lambda i: (0, 0, 0)), pl.BlockSpec((1, hidden), lambda i: (0, 0))]
        + [ANY] * len(needs),
        out_specs=[pl.BlockSpec((tm, hidden), lambda i: (i, 0))] * 2,
        out_shape=[jax.ShapeDtypeStruct((2 * tokens, hidden), BF)] * 2,
        compiler_params=pltpu.CompilerParams(vmem_limit_bytes=VMEM_BYTES),
        cost_estimate=SMALL,
        name="hidden_up",
    )(*x, *dy, w, b, *needs)


def down_kernel(*refs, half, step):
    la, lb, wa, wb = refs[:4]
    own, other = refs[-2:]

    def go(o):
        for j in range(0, o.shape[1], step):
            c = slice(j, j + step)
            o[:, c] = (dot_t(la[...], wa[0, c, :]) + dot_t(lb[...], wb[0, c, :])).astype(o.dtype)

    pl.when(pl.program_id(0) < half)(lambda: go(own))
    pl.when(pl.program_id(0) >= half)(lambda: go(other))


def down(left, weights, which, *needs):
    rows, hidden = left[0].shape
    width = weights[0].shape[1]
    half = 2
    tm = rows // 4
    lefts = pl.BlockSpec((tm, hidden), lambda i: (i, 0))
    ws = pl.BlockSpec((1, width, hidden), lambda i: (which, 0, 0))
    return pl.pallas_call(
        functools.partial(down_kernel, half=half, step=512),
        grid=(2 * half,),
        in_specs=[lefts, lefts, ws, ws] + [ANY] * len(needs),
        out_specs=[
            pl.BlockSpec((tm, width), lambda i: (jnp.minimum(i, half - 1), 0)),
            pl.BlockSpec((tm, width), lambda i: (jnp.maximum(i - half, 0), 0)),
        ],
        out_shape=[jax.ShapeDtypeStruct((rows // 2, width), F32), jax.ShapeDtypeStruct((rows // 2, width), BF)],
        compiler_params=pltpu.CompilerParams(vmem_limit_bytes=VMEM_BYTES),
        cost_estimate=SMALL,
        name="hidden_down",
    )(*left, *weights, *needs)


def grads_kernel(*refs):
    xs, ys, dus, gs, o_ref = refs[:4], refs[4:8], refs[8:10], refs[10:12], refs[-1]

    def go(left, right):
        lhs = jnp.concatenate([r[...] for r in left], axis=0)
        rhs = jnp.concatenate([r[...] for r in right], axis=0)
        o_ref[0] = dot_0(lhs, rhs).astype(BF)

    pl.when(pl.program_id(0) == 0)(lambda: go(xs, dus))
    pl.when(pl.program_id(0) == 1)(lambda: go(ys, gs))


def weight_grads(x, dy, du, g, *needs):
    tokens, width = x[0].shape
    hidden = du[0].shape[1]
    tm = min(256, width)
    last = width // tm - 1
    xs = pl.BlockSpec((tokens, tm), lambda j, i: (0, jnp.where(j == 0, i, last)))
    ys = pl.BlockSpec((tokens, tm), lambda j, i: (0, jnp.where(j == 0, 0, i)))
    rs = pl.BlockSpec((2 * tokens, hidden), lambda j, i: (0, 0))
    return pl.pallas_call(
        grads_kernel,
        grid=(2, width // tm),
        in_specs=[xs] * 4 + [ys] * 4 + [rs] * 4 + [ANY] * len(needs),
        out_specs=pl.BlockSpec((1, tm, hidden), lambda j, i: (j, i, 0)),
        out_shape=jax.ShapeDtypeStruct((2, width, hidden), BF),
        compiler_params=pltpu.CompilerParams(vmem_limit_bytes=VMEM_BYTES),
        cost_estimate=SMALL,
        name="hidden_grads",
    )(*x, *dy, *du, *g, *needs)


def normalise(x):
    mean = jnp.mean(x, axis=1, keepdims=True)
    cent = x - mean
    inv = lax.rsqrt(jnp.mean(cent * cent, axis=1, keepdims=True) + EPSILON)
    return mean, inv


def norm_back(grad, xhat, inv, gain):
    c = grad * gain
    return inv * (c - jnp.mean(c, axis=1, keepdims=True) - xhat * jnp.mean(c * xhat, axis=1, keepdims=True))


def gelu_both(u):
    k, a = math.sqrt(2 / math.pi), 0.044715
    square = u * u
    t = jnp.tanh(u * (k + (k * a) * square))
    h = 0.5 * (1 + t)
    return u * h, h + (0.5 * u) * (1 - t * t) * (k + (3 * k * a) * square)


def on_device(
    block_input,
    cotangent,
    attn_gain,
    attn_shift,
    query_weight,
    query_bias,
    keyval_weight,
    value_bias,
    output_weight,
    output_bias,
    mlp_gain,
    mlp_shift,
    expand_weight,
    expand_bias,
    shrink_weight,
    shrink_bias,
    seg_parent,
    seg_start,
    seg_length,
):
    rows, cols = lax.axis_size("row"), lax.axis_size("col")
    core, me, z = lax.axis_index("dp"), lax.axis_index("row"), lax.axis_index("col")
    local, feat = block_input.shape
    width = feat * rows
    tokens = local // rows
    bs = math.gcd(tokens, 128)
    blocks = tokens // bs
    eh = query_weight.shape[1] // 2
    fh = expand_weight.shape[1] // 2
    order = (0, 2, 1, 3)

    def send(x, axis, bits):
        n = lax.axis_size(axis)
        return lax.ppermute(x, axis, [(i, i ^ bits) for i in range(n)])

    swap = lambda x: send(x, "dp", 1)
    z_one = lambda x: send(x, "col", 1)
    z_two = lambda x: send(x, "col", 2)
    half_of = lambda x, c, size, axis: lax.dynamic_slice_in_dim(x, c * size, size, axis)

    def absolute(parts, index):
        bit = 1
        while bit < len(parts):
            odd = (index & bit) != 0
            parts = [jnp.where(odd, parts[j ^ bit], parts[j]) for j in range(len(parts))]
            bit *= 2
        return parts

    def to_rows(x, needs=(), then=()):
        x = x.reshape(blocks, rows, bs, feat)
        parts = [lax.dynamic_index_in_dim(x, me ^ k, 1, False).reshape(tokens, feat) for k in range(rows)]
        if needs:
            parts = hold(parts, *needs)
        parts = parts[:1] + [send(parts[k], "row", k) for k in range(1, rows)]
        return parts if needs else jnp.concatenate(absolute(parts, me), axis=1)

    def from_rows(x):
        piece = lambda k: half_of(x, me ^ k, feat, 1)
        parts = [piece(0)] + [send(piece(k), "row", k) for k in range(1, rows)]
        parts = [p.reshape(blocks, 1, bs, feat) for p in absolute(parts, me)]
        return jnp.concatenate(parts, axis=1).reshape(local, feat)

    def by_core(own, other, axis):
        return jnp.where(
            core == 0, jnp.concatenate([own, other], axis), jnp.concatenate([other, own], axis)
        )

    x_low = to_rows(block_input)
    x = x_low.astype(F32)

    vectors = jnp.stack([attn_gain, attn_shift, output_bias, mlp_gain, mlp_shift, shrink_bias] + [attn_gain] * 2)
    packed = jnp.concatenate([keyval_weight, vectors.reshape(-1, 2 * HD)], axis=0)
    packed = [packed] + [send(packed, "row", k) for k in range(1, rows)]
    packs = packed[1:]
    packed = jnp.stack(absolute(packed, me))
    up_bias = half_of(expand_bias, core, fh, 0).astype(F32)[None]
    up_bias = [up_bias, z_two(up_bias)]
    kv_weight = packed[:, :feat].reshape(width, 2 * HD)
    vectors = packed[:, feat:].reshape(rows, 8, feat).transpose(1, 0, 2).reshape(8, width).astype(F32)
    gain_one, shift_one, out_bias, gain_two, shift_two, down_bias = (vectors[i : i + 1] for i in range(6))

    gather_rows = lambda w, axis=0: lax.all_gather(w, "row", axis=axis, tiled=True)

    def four(block):
        return [block] + [send(block, "col", k) for k in order[1:]]

    q_bias = jnp.concatenate([jnp.stack(four(query_bias)).reshape(cols, 2, eh)], axis=0).astype(F32)
    q_bias = [lax.dynamic_index_in_dim(q_bias, c, 1, False).reshape(1, cols * eh) for c in (core, 1 - core)]

    def gather_square(four_blocks):
        own = gather_rows(jnp.concatenate(four_blocks, axis=1))
        return own, swap(own)

    query_blocks = four(half_of(query_weight, core, eh, 1))
    out_blocks = four(half_of(output_weight, core, eh, 0).T)
    query_blocks[1:] = hold(query_blocks[1:], x_low, up_bias[1], *packs)
    wq = gather_square(query_blocks)
    dy_parts = to_rows(cotangent, [x_low])

    hidden = jnp.stack([half_of(expand_weight, core, fh, 1), half_of(shrink_weight, core, fh, 0).T])

    hidden_z = z_two(hidden)

    mean_one, inv_one = normalise(x)
    normed = ((x - mean_one) * inv_one * gain_one + shift_one).astype(BF)
    kv_shift = jnp.concatenate([jnp.zeros((HD,), F32), value_bias.astype(F32)])[None]
    kv = (dot(normed, kv_weight) + kv_shift).astype(BF)
    out_blocks[1:] = hold(out_blocks[1:], kv)
    wo_t = gather_square(out_blocks)
    odd = z % 2
    kv_pair = jnp.stack(absolute([kv, z_one(kv)], odd))
    halves = [[kv_pair[:, : tokens // 2]], [kv_pair[:, tokens // 2 :]]]
    bits = [1 << i for i in range(rows.bit_length() - 1)]
    for step in range(len(bits)):
        for h, turn in ((0, bits), (1, bits[::-1])):
            halves[h] = halves[h] + [send(p, "row", turn[step]) for p in halves[h]]
    flip = lambda turn: [sum(turn[b] for b in range(len(bits)) if (i >> b) & 1) for i in range(rows)]
    for h, turn in ((0, bits), (1, bits[::-1])):
        held = flip(turn)
        halves[h] = jnp.stack(absolute([halves[h][held.index(k)] for k in range(rows)], me))
    kv_all = jnp.concatenate(halves, axis=2)
    kv_all = kv_all.reshape(rows, 2, blocks, bs, 2 * HD).transpose(1, 2, 0, 3, 4).reshape(2 * local, 2 * HD)
    keys, values = kv_all[:, :HD], kv_all[:, HD:]
    hidden_near = hold([half_of(expand_weight, core, fh, 1), half_of(shrink_weight, core, fh, 0).T], out_blocks[1])
    hidden_near = gather_rows(jnp.stack(hidden_near), 1)
    q = [(dot(normed, w) + v).astype(BF) for w, v in zip(wq, q_bias)]

    dy = jnp.concatenate(absolute(dy_parts, me), axis=1)
    dy_far = z_one(dy)

    tree = z // 2
    tree_row = lambda t: lax.dynamic_index_in_dim(t, tree, 0, False)
    places = odd * local + (jnp.arange(blocks, dtype=jnp.int32) * rows + me) * bs
    tab = block_table(tree_row(seg_parent), tree_row(seg_start), places)
    v_ext = jnp.concatenate([values, jnp.ones_like(values)], axis=1)
    *att, lse = attention_forward(tab, q, keys, v_ext, blocks, dy)
    (hidden_z,) = hold([hidden_z], att[0])
    hidden_w = [hidden_near, gather_rows(hidden_z, 1)]
    mid = x + dot_t(att[0], wo_t[0]) + dot_t(att[1], wo_t[1]) + out_bias

    mean_two, inv_two = normalise(mid)
    xhat_two = (mid - mean_two) * inv_two
    normed_two = (xhat_two * gain_two + shift_two).astype(BF)
    n2_far = z_one(normed_two)
    n2 = [(normed_two, swap(normed_two)), None]
    dy_all = [(dy, swap(dy)), None]
    act, dpre = [[None] * 2, [None] * 2], [[None] * 2, [None] * 2]
    scatter_rows = lambda w, axis=0: lax.psum_scatter(w, "row", scatter_dimension=axis, tiled=True)
    grads, last = [None] * 2, []
    for c in range(2):
        for a in range(2):
            act[a][c], dpre[a][c] = up(n2[a], dy_all[a], hidden_w[c], up_bias[c], *last)
            last = [dpre[a][c]]
            if n2[1] is None:
                n2_far, dy_far = hold([n2_far, dy_far], dpre[0][0])
                n2[1] = (n2_far, swap(n2_far))
                dy_all[1] = (dy_far, swap(dy_far))
        if c == 1:
            dn2_own, dn2_other = down(dpre[1], hidden_w, 0)
            dn2_far = (dn2_own + swap(dn2_other).astype(F32)).astype(BF)
            dn2_own, dn2_other = down(dpre[0], hidden_w, 0, dn2_own)
            (dn2_far,) = hold([dn2_far], dn2_own)
            last = [dn2_far]
            dn2_far = z_one(dn2_far)
        grads[c] = weight_grads(n2[0] + n2[1], dy_all[0] + dy_all[1], [d[c] for d in dpre], [g[c] for g in act], *last)
        last = [grads[c]]
    d_hidden_near = scatter_rows(grads[0], 1)
    (grads[1],) = hold([grads[1]], d_hidden_near)
    d_hidden_far = scatter_rows(grads[1], 1)
    branch_own, branch_other = down(act[1], hidden_w, 1, grads[1])
    near_own, near_other = down(act[0], hidden_w, 1, branch_own)
    (dn2_far,) = hold([dn2_far], near_own)
    dn2 = dn2_own + swap(dn2_other).astype(F32) + dn2_far.astype(F32)
    (branch_far,) = hold([(branch_own + swap(branch_other).astype(F32)).astype(BF)], dn2_far)
    branch_far = z_one(branch_far)
    branch_near = near_own + swap(near_other).astype(F32)

    dmid = dy.astype(F32) + norm_back(dn2, xhat_two, inv_two, gain_two)
    dmid_low = dmid.astype(BF)
    datt = [dot(dmid_low, w, BF) for w in wo_t]

    def halve(x, axis, mesh_axis, bits):
        parts = jnp.split(x, len(bits), axis=axis)
        got = [send(p, mesh_axis, b) for p, b in zip(parts[1:], bits[1:])]
        return sum((g.astype(F32) for g in got), parts[0].astype(F32)).astype(BF)

    def square_part(left, right):
        other = dot_0(left, right[1], BF)
        return (dot_0(left, right[0]) + swap(other).astype(F32)).astype(BF), other

    d_out = scatter_rows(square_part(dmid_low, att)[0])
    cut = blocks - 1
    *dq_a, dkv_part = attention_backward(tab, q, datt, att, lse, keys, values, blocks, 0, cut, None, d_hidden_far)
    (branch_far,) = hold([branch_far], dq_a[0])
    d_hidden_got = z_two(d_hidden_far)
    *dq_b, dkv_part = attention_backward(tab, q, datt, att, lse, keys, values, blocks, cut, blocks - cut, dkv_part, d_hidden_got)
    dq = [jnp.concatenate([u, v]) for u, v in zip(dq_a, dq_b)]
    d_hidden = d_hidden_near.astype(F32) + d_hidden_got.astype(F32)
    d_hidden = d_hidden.astype(BF)
    d_up, d_down = d_hidden[0], d_hidden[1]
    expand_weight_grad = by_core(d_up, swap(d_up), 1).astype(F32)
    shrink_weight_grad = by_core(d_down.T, swap(d_down.T), 0).astype(F32)

    branch = branch_near + branch_far.astype(F32)
    block_output = from_rows((mid + branch + down_bias).astype(BF))
    d_query, d_query_other = square_part(normed, dq)
    d_query = scatter_rows(d_query)
    parts = dkv_part.astype(BF).reshape(2, blocks, rows, bs, 2 * HD)
    pair = lambda k: lax.dynamic_index_in_dim(parts, odd ^ k, 0, False)
    dkv_sum = pair(0).astype(F32) + z_one(pair(1)).astype(F32)
    dkv_sum = dkv_sum.astype(BF)
    relative = lambda k: lax.dynamic_index_in_dim(dkv_sum, me ^ k, 1, False).reshape(tokens, 2 * HD)
    done = []
    for h, turn in ((0, bits), (1, bits[::-1])):
        cut = slice(h * tokens // 2, (h + 1) * tokens // 2)
        held = [relative(k)[cut] for k in flip(turn[::-1])]
        for step in range(len(bits)):
            n = len(held) // 2
            got = [send(p, "row", turn[::-1][len(bits) - 1 - step]) for p in held[n:]]
            held = [(p.astype(F32) + g.astype(F32)).astype(BF) for p, g in zip(held[:n], got)]
        done.append(held[0])
    dkv = jnp.concatenate(done, axis=0)
    (d_out,) = hold([d_out], dkv)
    d_out = halve(d_out, 1, "col", order)
    output_weight_grad = by_core(d_out.T, swap(d_out.T), 0).astype(F32)
    d_query = halve(d_query, 1, "col", order)
    query_weight_grad = by_core(d_query, swap(d_query), 1).astype(F32)

    (dkv,) = hold([dkv], block_output)
    dn1 = dot_t(dq[0], wq[0]) + dot_t(dq[1], wq[1]) + dot_t(dkv, kv_weight)
    xhat_one = (x - mean_one) * inv_one
    input_grad = (dmid + norm_back(dn1, xhat_one, inv_one, gain_one)).astype(BF)
    (dkv,) = hold([dkv], input_grad)
    input_grad = from_rows(input_grad).astype(F32)

    total = lambda t: jnp.sum(t.astype(F32), axis=0)
    fill = -feat % (2 * HD)
    place = lambda v: jnp.pad(v.reshape(rows, feat), ((0, 0), (0, fill))).reshape(rows, -1, 2 * HD)
    same = lambda v: jnp.broadcast_to(v.reshape(1, -1, 2 * HD), (rows, v.size // (2 * HD), 2 * HD))
    dq_sum = jnp.stack([total(dq[0]), total(dq[1])]).reshape(2, cols, eh)
    dq_sum = absolute([dq_sum[:, order.index(k)] for k in range(cols)], z)
    dq_sum = jnp.stack([jnp.stack(absolute([d[0], d[1]], core)) for d in dq_sum]).reshape(-1)
    up_sums = [total(dpre[0][c]) + total(dpre[1][c]) for c in (0, 1)]
    zero = jnp.zeros_like(up_sums[0])
    up_sums = absolute([up_sums[0], zero, up_sums[1], zero], z)
    up_sums = jnp.stack([jnp.stack(absolute([u, zero], core)) for u in up_sums]).reshape(-1)
    v_sum = jnp.concatenate([total(dkv[:, HD:]), jnp.zeros((HD,), F32)])
    vecs = [place(total(dn1 * xhat_one)), place(total(dn1)), place(total(dn2 * xhat_two)), place(total(dn2)),
            place(total(dmid_low)), place(total(dy)), same(dq_sum), same(up_sums), same(v_sum)]
    sizes = [v.shape[1] for v in vecs]
    pad = -sum(sizes) % 16
    vecs.append(jnp.zeros((rows, pad, 2 * HD), F32))
    packs = [dot_0(normed, dkv, BF).reshape(rows, feat, 2 * HD), jnp.concatenate(vecs, axis=1).astype(BF)]
    add_up = lambda first, others: sum((o.astype(F32) for o in others), first.astype(F32)).astype(BF)
    for i, pack in enumerate(packs):
        held = [lax.dynamic_index_in_dim(pack, me ^ k, 0, False) for k in range(rows)]
        pack = add_up(held[0], [send(held[k], "row", k) for k in range(1, rows)])
        pack = add_up(pack, [swap(pack)])
        packs[i] = add_up(pack, [send(pack, "col", k) for k in range(1, cols)])
    keyval_weight_grad = packs[0].astype(F32)
    pack = packs[1]
    ends, at = [], 0
    for n in sizes:
        ends.append(pack[at : at + n].astype(F32).reshape(-1))
        at += n
    return (
        block_output,
        input_grad,
        ends[0][:feat],
        ends[1][:feat],
        query_weight_grad,
        half_of(ends[6], z, 2 * eh, 0),
        keyval_weight_grad,
        ends[8][:HD],
        output_weight_grad,
        ends[4][:feat],
        ends[2][:feat],
        ends[3][:feat],
        expand_weight_grad,
        half_of(ends[7], z, 2 * fh, 0),
        shrink_weight_grad,
        ends[5][:feat],
    )


def solution(mesh):
    tokens, row, col = P(("dp", "col"), "row"), P("row"), P("col")
    tree = P("dp", None)
    return jax.shard_map(
        on_device,
        mesh=mesh,
        in_specs=(
            tokens, tokens, row, row, P("row", "col"), col, P("row", None), P(), P("col", "row"), row,
            row, row, P("row", "col"), col, P("col", "row"), row, tree, tree, tree,
        ),
        out_specs=(
            tokens, tokens, row, row, P("row", "col"), col, P("row", None), P(), P("col", "row"), row,
            row, row, P("row", "col"), col, P("col", "row"), row,
        ),
        check_vma=False,
    )
```

```python
import functools
import math

import jax
import jax.numpy as jnp
from jax import lax
from jax.experimental import pallas as pl
from jax.experimental.pallas import tpu as pltpu
from jax.sharding import PartitionSpec as P

HD = 128
TREE_TOK = 5120
TRUNK = 2048
EPSILON = 1e-05
SCALE = HD**-0.5
SCALE2 = SCALE * math.log2(math.e)
NEG = -1e30
TILE = 512
BF = jnp.bfloat16
F32 = jnp.float32
VMEM_BYTES = 60 * 1024 * 1024


def dot(a, b, out=F32):
    return jnp.dot(a, b, preferred_element_type=F32).astype(out)


def dot_t(a, b, out=F32):
    return lax.dot_general(a, b, (((1,), (1,)), ((), ())), preferred_element_type=F32).astype(out)


def dot_0(a, b, out=F32):
    return lax.dot_general(a, b, (((0,), (0,)), ((), ())), preferred_element_type=F32).astype(out)


def tail_rows(tab, i):
    return pl.ds(pl.multiple_of(tab[2, i], 128), TILE // 2), pl.ds(
        pl.multiple_of(tab[4, i], 128), TILE // 2
    )


def place_of(head, heads):
    half = heads // 2
    return head // half, slice(head % half * HD, (head % half + 1) * HD)


def fwd_kernel(tab, *refs, bs, heads, hg):
    qa_ref, qb_ref, k_ref, v_ref = refs[:4]
    oa_ref, ob_ref, lse_ref = refs[-3:]
    i = pl.program_id(0)
    full, base = tab[0, i], tab[1, i]
    lim0, lim1 = tab[3, i], tab[5, i]
    half = TILE // 2
    r0, r1 = tail_rows(tab, i)
    row = lax.broadcasted_iota(jnp.int32, (hg * bs, TILE), 0) & (bs - 1)
    col = lax.broadcasted_iota(jnp.int32, (hg * bs, TILE), 1)
    mask = col <= row + jnp.where(col < half, lim0, lim1 + half)
    for g in range(heads // hg):
        at = [place_of(g * hg + h, heads) for h in range(hg)]
        q = jnp.concatenate([(qa_ref, qb_ref)[w][:, c] for w, c in at], axis=0)
        kt = jnp.concatenate([k_ref[r0, :], k_ref[r1, :]], axis=0)
        vt = jnp.concatenate([v_ref[r0, :], v_ref[r1, :]], axis=0)
        s = jnp.where(mask, dot_t(q, kt) * SCALE2, NEG)
        top = jnp.max(s, axis=1, keepdims=True)
        acc = dot(jnp.exp2(s - top).astype(BF), vt)

        def body(t, carry):
            top, acc = carry
            rr = pl.ds(pl.multiple_of(base + t * TILE, 128), TILE)
            s = dot_t(q, k_ref[rr, :]) * SCALE2
            new = jnp.maximum(top, jnp.max(s, axis=1, keepdims=True))
            p = jnp.exp2(s - new).astype(BF)
            return new, acc * jnp.exp2(top - new) + dot(p, v_ref[rr, :])

        top, acc = lax.fori_loop(0, full, body, (top, acc))
        total = acc[:, HD:]
        out = (acc[:, :HD] / total).astype(BF)
        lse = top + jnp.log2(total)
        for h in range(hg):
            (oa_ref, ob_ref)[at[h][0]][:, at[h][1]] = out[h * bs : (h + 1) * bs]
            lse_ref[0, g * hg + h : g * hg + h + 1, :] = jnp.transpose(lse[h * bs : (h + 1) * bs])[0:1, :]


def attention_forward(tab, q, k, v_ext, blocks, *needs):
    tokens, width = q[0].shape
    bs, heads = tokens // blocks, 2 * width // HD
    qs = pl.BlockSpec((bs, width), lambda i, t: (i, 0))
    return pl.pallas_call(
        functools.partial(fwd_kernel, bs=bs, heads=heads, hg=heads),
        grid_spec=pltpu.PrefetchScalarGridSpec(
            num_scalar_prefetch=1,
            grid=(blocks,),
            in_specs=[
                qs,
                qs,
                pl.BlockSpec(k.shape, lambda i, t: (0, 0)),
                pl.BlockSpec(v_ext.shape, lambda i, t: (0, 0)),
            ]
            + [ANY] * len(needs),
            out_specs=[
                qs,
                qs,
                pl.BlockSpec((1, heads, bs), lambda i, t: (i, 0, 0)),
            ],
        ),
        out_shape=[
            jax.ShapeDtypeStruct((tokens, width), BF),
            jax.ShapeDtypeStruct((tokens, width), BF),
            jax.ShapeDtypeStruct((blocks, heads, bs), F32),
        ],
        compiler_params=pltpu.CompilerParams(vmem_limit_bytes=VMEM_BYTES),
        cost_estimate=SMALL,
        name="attn_fwd",
    )(tab, *q, k, v_ext, *needs)


def bwd_kernel(tab, *refs, bs, heads, hg, more):
    qa_ref, qb_ref, daa_ref, dab_ref, aa_ref, ab_ref, lse_ref, k_ref, v_ref = refs[:9]
    dqa_ref, dqb_ref, dkv_ref = refs[-3:]
    i = pl.program_id(0)
    full, base = tab[0, i], tab[1, i]
    lim0, lim1 = tab[3, i], tab[5, i]
    half = TILE // 2
    r0, r1 = tail_rows(tab, i)
    row = lax.broadcasted_iota(jnp.int32, (TILE, hg * bs), 1) & (bs - 1)
    col = lax.broadcasted_iota(jnp.int32, (TILE, hg * bs), 0)
    mask = col <= row + jnp.where(col < half, lim0, lim1 + half)

    @pl.when(i == 0)
    def _():
        dkv_ref[...] = refs[9][...] if more else jnp.zeros_like(dkv_ref)

    for g in range(heads // hg):
        at = [place_of(g * hg + h, heads) for h in range(hg)]
        q = jnp.concatenate([(qa_ref, qb_ref)[w][:, c] for w, c in at], axis=0)
        da = jnp.concatenate([(daa_ref, dab_ref)[w][:, c] for w, c in at], axis=0)
        lse = jnp.concatenate([lse_ref[0, g * hg + h : g * hg + h + 1, :] for h in range(hg)], axis=1)
        delta = jnp.concatenate(
            [
                jnp.sum(
                    jnp.transpose((daa_ref, dab_ref)[w][:, c].astype(F32) * (aa_ref, ab_ref)[w][:, c].astype(F32)),
                    axis=0,
                    keepdims=True,
                )
                for w, c in at
            ],
            axis=1,
        )

        def tile(kt, vt, visible):
            st = dot_t(kt, q) * SCALE2 - lse
            if visible is not None:
                st = jnp.where(visible, st, NEG)
            pt = jnp.exp2(st)
            dst = (pt * (dot_t(vt, da) - delta)).astype(BF)
            return dot(dst, q) * SCALE, dot(pt.astype(BF), da), dot_0(dst, kt)

        kt = jnp.concatenate([k_ref[r0, :], k_ref[r1, :]], axis=0)
        vt = jnp.concatenate([v_ref[r0, :], v_ref[r1, :]], axis=0)
        dk, dv, dq = tile(kt, vt, mask)
        dkv_ref[r0, :HD] += dk[:half]
        dkv_ref[r0, HD:] += dv[:half]
        dkv_ref[r1, :HD] += dk[half:]
        dkv_ref[r1, HD:] += dv[half:]

        def body(t, dq):
            rr = pl.ds(pl.multiple_of(base + t * TILE, 128), TILE)
            dk, dv, more = tile(k_ref[rr, :], v_ref[rr, :], None)
            dkv_ref[rr, :HD] += dk
            dkv_ref[rr, HD:] += dv
            return dq + more

        dq = (lax.fori_loop(0, full, body, dq) * SCALE).astype(BF)
        for h in range(hg):
            (dqa_ref, dqb_ref)[at[h][0]][:, at[h][1]] = dq[h * bs : (h + 1) * bs]


def attention_backward(tab, q, da, a, lse, k, v, blocks, first, count, so_far, *needs):
    tokens, width = q[0].shape
    bs, heads = tokens // blocks, 2 * width // HD
    qs = pl.BlockSpec((bs, width), lambda i, t: (i + first, 0))
    ks = pl.BlockSpec(k.shape, lambda i, t: (0, 0))
    whole = pl.BlockSpec((k.shape[0], 2 * HD), lambda i, t: (0, 0))
    out = pl.BlockSpec((bs, width), lambda i, t: (i, 0))
    more = [] if so_far is None else [so_far]
    return pl.pallas_call(
        functools.partial(bwd_kernel, bs=bs, heads=heads, hg=heads, more=bool(more)),
        grid_spec=pltpu.PrefetchScalarGridSpec(
            num_scalar_prefetch=1,
            grid=(count,),
            in_specs=[qs] * 6
            + [pl.BlockSpec((1, heads, bs), lambda i, t: (i + first, 0, 0)), ks, ks]
            + [whole] * len(more)
            + [ANY] * len(needs),
            out_specs=[out, out, whole],
        ),
        out_shape=[
            jax.ShapeDtypeStruct((count * bs, width), BF),
            jax.ShapeDtypeStruct((count * bs, width), BF),
            jax.ShapeDtypeStruct((k.shape[0], 2 * HD), F32),
        ],
        compiler_params=pltpu.CompilerParams(vmem_limit_bytes=VMEM_BYTES),
        cost_estimate=SMALL,
        name="attn_bwd",
    )(tab[:, first : first + count], *q, *da, *a, lse, k, v, *more, *needs)


def block_table(parent, start, places):
    slots = jnp.arange(parent.shape[0], dtype=jnp.int32)
    length = jnp.where(parent < 0, TRUNK, TILE // 2)
    mine = (places[:, None] >= start[None, :]) & (places[:, None] < (start + length)[None, :])
    pick = lambda sel, vals: jnp.sum(jnp.where(sel, vals[None, :], 0), axis=1)
    seg = pick(mine, slots)
    own = pick(mine, start)
    par = pick(mine, parent)
    is_par = slots[None, :] == par[:, None]
    par_start = pick(is_par, start)
    grand = jnp.where(par < 0, -1, pick(is_par, parent))
    trunk = jnp.sum(jnp.where(parent < 0, start, 0))
    off = places - own
    in_trunk, leaf = par < 0, grand >= 0
    full = jnp.where(in_trunk, off // TILE, TRUNK // TILE)
    half = TILE // 2
    first = jnp.where(in_trunk, trunk + full * TILE, jnp.where(leaf, par_start, own))
    lim_first = jnp.where(in_trunk, off - full * TILE, jnp.where(leaf, 2 * TILE, off))
    second = jnp.where(in_trunk, trunk + full * TILE + half, own)
    lim_second = jnp.where(in_trunk, off - full * TILE - half, jnp.where(leaf, off, -2 * TILE))
    return jnp.stack([full, jnp.full_like(full, trunk), first, lim_first, second, lim_second]).astype(jnp.int32)


SMALL = pl.CostEstimate(flops=1_000_000, bytes_accessed=1_000_000, transcendentals=0)
ANY = pl.BlockSpec(memory_space=pl.ANY)


def hold(values, *needs):
    values = list(values)
    n, m = len(values), len(needs)
    out = pl.pallas_call(
        lambda *refs: None,
        in_specs=[ANY] * (n + m),
        out_specs=[ANY] * n,
        out_shape=[jax.ShapeDtypeStruct(v.shape, v.dtype) for v in values],
        input_output_aliases={i: i for i in range(n)},
        cost_estimate=SMALL,
        name="hold",
    )(*values, *needs)
    return list(out)


def up_kernel(*refs, half, step):
    xa, xb, ya, yb, w, b = refs[:6]
    g_ref, du_ref = refs[-2:]

    def go(x, y):
        for j in range(0, w.shape[2], step):
            c = slice(j, j + step)
            u = dot(x[...], w[0, :, c]) + b[:, c]
            d = dot(y[...], w[1, :, c])
            g, slope = gelu_both(u)
            g_ref[:, c] = g.astype(BF)
            du_ref[:, c] = (d * slope).astype(BF)

    pl.when(pl.program_id(0) < half)(lambda: go(xa, ya))
    pl.when(pl.program_id(0) >= half)(lambda: go(xb, yb))


def up(x, dy, w, b, *needs):
    tokens, width = x[0].shape
    hidden = w.shape[2]
    tm, half = tokens // 2, 2
    first = pl.BlockSpec((tm, width), lambda i: (jnp.minimum(i, half - 1), 0))
    second = pl.BlockSpec((tm, width), lambda i: (jnp.maximum(i - half, 0), 0))
    return pl.pallas_call(
        functools.partial(up_kernel, half=half, step=512),
        grid=(2 * half,),
        in_specs=[first, second, first, second, pl.BlockSpec(w.shape, lambda i: (0, 0, 0)), pl.BlockSpec((1, hidden), lambda i: (0, 0))]
        + [ANY] * len(needs),
        out_specs=[pl.BlockSpec((tm, hidden), lambda i: (i, 0))] * 2,
        out_shape=[jax.ShapeDtypeStruct((2 * tokens, hidden), BF)] * 2,
        compiler_params=pltpu.CompilerParams(vmem_limit_bytes=VMEM_BYTES),
        cost_estimate=SMALL,
        name="hidden_up",
    )(*x, *dy, w, b, *needs)


def down_kernel(*refs, half, step):
    la, lb, wa, wb = refs[:4]
    own, other = refs[-2:]

    def go(o):
        for j in range(0, o.shape[1], step):
            c = slice(j, j + step)
            o[:, c] = (dot_t(la[...], wa[0, c, :]) + dot_t(lb[...], wb[0, c, :])).astype(o.dtype)

    pl.when(pl.program_id(0) < half)(lambda: go(own))
    pl.when(pl.program_id(0) >= half)(lambda: go(other))


def down(left, weights, which, *needs):
    rows, hidden = left[0].shape
    width = weights[0].shape[1]
    half = 2
    tm = rows // 4
    lefts = pl.BlockSpec((tm, hidden), lambda i: (i, 0))
    ws = pl.BlockSpec((1, width, hidden), lambda i: (which, 0, 0))
    return pl.pallas_call(
        functools.partial(down_kernel, half=half, step=512),
        grid=(2 * half,),
        in_specs=[lefts, lefts, ws, ws] + [ANY] * len(needs),
        out_specs=[
            pl.BlockSpec((tm, width), lambda i: (jnp.minimum(i, half - 1), 0)),
            pl.BlockSpec((tm, width), lambda i: (jnp.maximum(i - half, 0), 0)),
        ],
        out_shape=[jax.ShapeDtypeStruct((rows // 2, width), F32), jax.ShapeDtypeStruct((rows // 2, width), BF)],
        compiler_params=pltpu.CompilerParams(vmem_limit_bytes=VMEM_BYTES),
        cost_estimate=SMALL,
        name="hidden_down",
    )(*left, *weights, *needs)


def grads_kernel(*refs):
    xs, ys, dus, gs, o_ref = refs[:4], refs[4:8], refs[8:10], refs[10:12], refs[-1]

    def go(left, right):
        lhs = jnp.concatenate([r[...] for r in left], axis=0)
        rhs = jnp.concatenate([r[...] for r in right], axis=0)
        o_ref[0] = dot_0(lhs, rhs).astype(BF)

    pl.when(pl.program_id(0) == 0)(lambda: go(xs, dus))
    pl.when(pl.program_id(0) == 1)(lambda: go(ys, gs))


def weight_grads(x, dy, du, g, *needs):
    tokens, width = x[0].shape
    hidden = du[0].shape[1]
    tm = min(256, width)
    last = width // tm - 1
    xs = pl.BlockSpec((tokens, tm), lambda j, i: (0, jnp.where(j == 0, i, last)))
    ys = pl.BlockSpec((tokens, tm), lambda j, i: (0, jnp.where(j == 0, 0, i)))
    rs = pl.BlockSpec((2 * tokens, hidden), lambda j, i: (0, 0))
    return pl.pallas_call(
        grads_kernel,
        grid=(2, width // tm),
        in_specs=[xs] * 4 + [ys] * 4 + [rs] * 4 + [ANY] * len(needs),
        out_specs=pl.BlockSpec((1, tm, hidden), lambda j, i: (j, i, 0)),
        out_shape=jax.ShapeDtypeStruct((2, width, hidden), BF),
        compiler_params=pltpu.CompilerParams(vmem_limit_bytes=VMEM_BYTES),
        cost_estimate=SMALL,
        name="hidden_grads",
    )(*x, *dy, *du, *g, *needs)


def normalise(x):
    mean = jnp.mean(x, axis=1, keepdims=True)
    cent = x - mean
    inv = lax.rsqrt(jnp.mean(cent * cent, axis=1, keepdims=True) + EPSILON)
    return mean, inv


def norm_back(grad, xhat, inv, gain):
    c = grad * gain
    return inv * (c - jnp.mean(c, axis=1, keepdims=True) - xhat * jnp.mean(c * xhat, axis=1, keepdims=True))


def gelu_both(u):
    k, a = math.sqrt(2 / math.pi), 0.044715
    square = u * u
    t = jnp.tanh(u * (k + (k * a) * square))
    h = 0.5 * (1 + t)
    return u * h, h + (0.5 * u) * (1 - t * t) * (k + (3 * k * a) * square)


def on_device(
    block_input,
    cotangent,
    attn_gain,
    attn_shift,
    query_weight,
    query_bias,
    keyval_weight,
    value_bias,
    output_weight,
    output_bias,
    mlp_gain,
    mlp_shift,
    expand_weight,
    expand_bias,
    shrink_weight,
    shrink_bias,
    seg_parent,
    seg_start,
    seg_length,
):
    rows, cols = lax.axis_size("row"), lax.axis_size("col")
    core, me, z = lax.axis_index("dp"), lax.axis_index("row"), lax.axis_index("col")
    local, feat = block_input.shape
    width = feat * rows
    tokens = local // rows
    bs = math.gcd(tokens, 128)
    blocks = tokens // bs
    eh = query_weight.shape[1] // 2
    fh = expand_weight.shape[1] // 2
    order = (0, 2, 1, 3)

    def send(x, axis, bits):
        n = lax.axis_size(axis)
        return lax.ppermute(x, axis, [(i, i ^ bits) for i in range(n)])

    swap = lambda x: send(x, "dp", 1)
    z_one = lambda x: send(x, "col", 1)
    z_two = lambda x: send(x, "col", 2)
    half_of = lambda x, c, size, axis: lax.dynamic_slice_in_dim(x, c * size, size, axis)

    def absolute(parts, index):
        bit = 1
        while bit < len(parts):
            odd = (index & bit) != 0
            parts = [jnp.where(odd, parts[j ^ bit], parts[j]) for j in range(len(parts))]
            bit *= 2
        return parts

    def to_rows(x, needs=(), then=()):
        x = x.reshape(blocks, rows, bs, feat)
        parts = [lax.dynamic_index_in_dim(x, me ^ k, 1, False).reshape(tokens, feat) for k in range(rows)]
        if needs:
            parts = hold(parts, *needs)
        parts = parts[:1] + [send(parts[k], "row", k) for k in range(1, rows)]
        return parts

    def from_rows(x):
        piece = lambda k: half_of(x, me ^ k, feat, 1)
        parts = [piece(0)] + [send(piece(k), "row", k) for k in range(1, rows)]
        parts = [p.reshape(blocks, 1, bs, feat) for p in absolute(parts, me)]
        return jnp.concatenate(parts, axis=1).reshape(local, feat)

    def by_core(own, other, axis):
        return jnp.where(
            core == 0, jnp.concatenate([own, other], axis), jnp.concatenate([other, own], axis)
        )

    x_parts = to_rows(block_input)
    x_low = jnp.concatenate(absolute(x_parts, me), axis=1)
    x = x_low.astype(F32)

    vectors = jnp.stack([attn_gain, attn_shift, output_bias, mlp_gain, mlp_shift, shrink_bias] + [attn_gain] * 2)
    packed = jnp.concatenate([keyval_weight, vectors.reshape(-1, 2 * HD)], axis=0)
    packed = [packed] + [send(packed, "row", k) for k in range(1, rows)]
    packs = packed[1:]
    packed = jnp.stack(absolute(packed, me))
    up_bias = half_of(expand_bias, core, fh, 0).astype(F32)[None]
    up_bias = [up_bias, z_two(up_bias)]
    kv_weight = packed[:, :feat].reshape(width, 2 * HD)
    vectors = packed[:, feat:].reshape(rows, 8, feat).transpose(1, 0, 2).reshape(8, width).astype(F32)
    gain_one, shift_one, out_bias, gain_two, shift_two, down_bias = (vectors[i : i + 1] for i in range(6))

    gather_rows = lambda w, axis=0: lax.all_gather(w, "row", axis=axis, tiled=True)

    def four(block):
        return [block] + [send(block, "col", k) for k in order[1:]]

    q_parts = four(query_bias)
    q_bias = jnp.stack(q_parts).reshape(cols, 2, eh).astype(F32)
    q_bias = [lax.dynamic_index_in_dim(q_bias, c, 1, False).reshape(1, cols * eh) for c in (core, 1 - core)]

    def gather_square(four_blocks):
        own = gather_rows(jnp.concatenate(four_blocks, axis=1))
        return own, swap(own)

    query_blocks = four(half_of(query_weight, core, eh, 1))
    out_blocks = four(half_of(output_weight, core, eh, 0).T)
    hidden = jnp.stack([half_of(expand_weight, core, fh, 1), half_of(shrink_weight, core, fh, 0).T])
    pieces = [z_two(p) for p in jnp.split(hidden, 8, axis=2)]
    query_blocks[1:] = hold(query_blocks[1:], x_parts[-1], pieces[0])
    wq_own = gather_rows(jnp.concatenate(query_blocks, axis=1))
    dy_parts = to_rows(cotangent, [x_low])


    mean_one, inv_one = normalise(x)
    normed = ((x - mean_one) * inv_one * gain_one + shift_one).astype(BF)
    kv_shift = jnp.concatenate([jnp.zeros((HD,), F32), value_bias.astype(F32)])[None]
    kv = (dot(normed, kv_weight) + kv_shift).astype(BF)
    out_blocks[1:] = hold(out_blocks[1:], kv, up_bias[1], pieces[1], *q_parts[1:])
    wo_t = gather_square(out_blocks)
    odd = z % 2
    kv_pair = jnp.stack(absolute([kv, z_one(kv)], odd))
    halves = hold([kv_pair[:, : tokens // 2], kv_pair[:, tokens // 2 :]], pieces[2], dy_parts[-1])
    halves = [[h] for h in halves]
    bits = [1 << i for i in range(rows.bit_length() - 1)]
    for step in range(len(bits)):
        for h, turn in ((0, bits), (1, bits[::-1])):
            halves[h] = halves[h] + [send(p, "row", turn[step]) for p in halves[h]]
        if step == 0:
            n = len(halves[0])
            both = hold(halves[0] + halves[1], pieces[3], dy_parts[1])
            halves = [both[:n], both[n:]]
    flip = lambda turn: [sum(turn[b] for b in range(len(bits)) if (i >> b) & 1) for i in range(rows)]
    for h, turn in ((0, bits), (1, bits[::-1])):
        held = flip(turn)
        halves[h] = jnp.stack(absolute([halves[h][held.index(k)] for k in range(rows)], me))
    kv_all = jnp.concatenate(halves, axis=2)
    kv_all = kv_all.reshape(rows, 2, blocks, bs, 2 * HD).transpose(1, 2, 0, 3, 4).reshape(2 * local, 2 * HD)
    keys, values = kv_all[:, :HD], kv_all[:, HD:]
    hidden_near = hold([half_of(expand_weight, core, fh, 1), half_of(shrink_weight, core, fh, 0).T], out_blocks[1])
    hidden_near = gather_rows(jnp.stack(hidden_near), 1)
    (wq_own,) = hold([wq_own], keys, pieces[4], *dy_parts[2:-1])
    wq = [wq_own, swap(wq_own)]
    q = [(dot(normed, w) + v).astype(BF) for w, v in zip(wq, q_bias)]

    dy = jnp.concatenate(absolute(dy_parts, me), axis=1)
    dy_far = z_one(dy)

    tree = z // 2
    tree_row = lambda t: lax.dynamic_index_in_dim(t, tree, 0, False)
    places = odd * local + (jnp.arange(blocks, dtype=jnp.int32) * rows + me) * bs
    tab = block_table(tree_row(seg_parent), tree_row(seg_start), places)
    v_ext = jnp.concatenate([values, jnp.ones_like(values)], axis=1)
    *att, lse = attention_forward(tab, q, keys, v_ext, blocks, dy, pieces[5])
    *pieces[6:], dy_far = hold(pieces[6:] + [dy_far], att[0])
    hidden_z = jnp.concatenate(pieces, axis=2)
    hidden_w = [hidden_near, gather_rows(hidden_z, 1)]
    mid = x + dot_t(att[0], wo_t[0]) + dot_t(att[1], wo_t[1]) + out_bias

    mean_two, inv_two = normalise(mid)
    xhat_two = (mid - mean_two) * inv_two
    normed_two = (xhat_two * gain_two + shift_two).astype(BF)
    n2_far = z_one(normed_two)
    n2 = [(normed_two, swap(normed_two)), None]
    dy_all = [(dy, swap(dy)), None]
    act, dpre = [[None] * 2, [None] * 2], [[None] * 2, [None] * 2]
    scatter_rows = lambda w, axis=0: lax.psum_scatter(w, "row", scatter_dimension=axis, tiled=True)
    grads, last = [None] * 2, []
    for c in range(2):
        for a in range(2):
            act[a][c], dpre[a][c] = up(n2[a], dy_all[a], hidden_w[c], up_bias[c], *last)
            last = [dpre[a][c]]
            if n2[1] is None:
                (n2_far,) = hold([n2_far], dpre[0][0])
                n2[1] = (n2_far, swap(n2_far))
                dy_all[1] = (dy_far, swap(dy_far))
        if c == 1:
            dn2_own, dn2_other = down(dpre[1], hidden_w, 0)
            dn2_far = (dn2_own + swap(dn2_other).astype(F32)).astype(BF)
            dn2_own, dn2_other = down(dpre[0], hidden_w, 0, dn2_own)
            (dn2_far,) = hold([dn2_far], dn2_own)
            last = [dn2_far]
            dn2_far = z_one(dn2_far)
        grads[c] = weight_grads(n2[0] + n2[1], dy_all[0] + dy_all[1], [d[c] for d in dpre], [g[c] for g in act], *last)
        last = [grads[c]]
    d_hidden_near = scatter_rows(grads[0], 1)
    (grads[1],) = hold([grads[1]], d_hidden_near)
    d_hidden_far = scatter_rows(grads[1], 1)
    branch_own, branch_other = down(act[1], hidden_w, 1, grads[1])
    near_own, near_other = down(act[0], hidden_w, 1, branch_own)
    (dn2_far,) = hold([dn2_far], near_own)
    dn2 = dn2_own + swap(dn2_other).astype(F32) + dn2_far.astype(F32)
    (branch_far,) = hold([(branch_own + swap(branch_other).astype(F32)).astype(BF)], dn2_far)
    branch_far = z_one(branch_far)
    branch_near = near_own + swap(near_other).astype(F32)

    dmid = dy.astype(F32) + norm_back(dn2, xhat_two, inv_two, gain_two)
    dmid_low = dmid.astype(BF)
    datt = [dot(dmid_low, w, BF) for w in wo_t]

    def halve(x, axis, mesh_axis, bits):
        parts = jnp.split(x, len(bits), axis=axis)
        got = [send(p, mesh_axis, b) for p, b in zip(parts[1:], bits[1:])]
        return sum((g.astype(F32) for g in got), parts[0].astype(F32)).astype(BF)

    def square_part(left, right):
        other = dot_0(left, right[1], BF)
        return (dot_0(left, right[0]) + swap(other).astype(F32)).astype(BF), other

    d_out = scatter_rows(square_part(dmid_low, att)[0])
    cut = blocks - 1
    *dq_a, dkv_part = attention_backward(tab, q, datt, att, lse, keys, values, blocks, 0, cut, None, d_hidden_far)
    d_hidden_got = z_two(d_hidden_far)
    *dq_b, dkv_part = attention_backward(tab, q, datt, att, lse, keys, values, blocks, cut, blocks - cut, dkv_part, d_hidden_got)
    dq = [jnp.concatenate([u, v]) for u, v in zip(dq_a, dq_b)]
    d_hidden = d_hidden_near.astype(F32) + d_hidden_got.astype(F32)
    d_hidden = d_hidden.astype(BF)
    d_up, d_down = d_hidden[0], d_hidden[1]
    expand_weight_grad = by_core(d_up, swap(d_up), 1).astype(F32)
    shrink_weight_grad = by_core(d_down.T, swap(d_down.T), 0).astype(F32)

    (branch_far,) = hold([branch_far], dq_b[0])
    branch = branch_near + branch_far.astype(F32)
    block_output = from_rows((mid + branch + down_bias).astype(BF))
    d_query, d_query_other = square_part(normed, dq)
    d_query = scatter_rows(d_query)
    parts = dkv_part.astype(BF).reshape(2, blocks, rows, bs, 2 * HD)
    pair = lambda k: lax.dynamic_index_in_dim(parts, odd ^ k, 0, False)
    dkv_sum = pair(0).astype(F32) + z_one(pair(1)).astype(F32)
    dkv_sum = dkv_sum.astype(BF)
    relative = lambda k: lax.dynamic_index_in_dim(dkv_sum, me ^ k, 1, False).reshape(tokens, 2 * HD)
    done = []
    for h, turn in ((0, bits), (1, bits[::-1])):
        cut = slice(h * tokens // 2, (h + 1) * tokens // 2)
        held = [relative(k)[cut] for k in flip(turn[::-1])]
        for step in range(len(bits)):
            n = len(held) // 2
            got = [send(p, "row", turn[::-1][len(bits) - 1 - step]) for p in held[n:]]
            held = [(p.astype(F32) + g.astype(F32)).astype(BF) for p, g in zip(held[:n], got)]
        done.append(held[0])
    dkv = jnp.concatenate(done, axis=0)
    (d_out,) = hold([d_out], dkv)
    d_out = halve(d_out, 1, "col", order)
    output_weight_grad = by_core(d_out.T, swap(d_out.T), 0).astype(F32)
    d_query = halve(d_query, 1, "col", order)
    query_weight_grad = by_core(d_query, swap(d_query), 1).astype(F32)

    (dkv,) = hold([dkv], block_output)
    dn1 = dot_t(dq[0], wq[0]) + dot_t(dq[1], wq[1]) + dot_t(dkv, kv_weight)
    xhat_one = (x - mean_one) * inv_one
    input_grad = (dmid + norm_back(dn1, xhat_one, inv_one, gain_one)).astype(BF)
    add_up = lambda first, others: sum((o.astype(F32) for o in others), first.astype(F32)).astype(BF)

    def over_row(pack):
        held = [lax.dynamic_index_in_dim(pack, me ^ k, 0, False) for k in range(rows)]
        return add_up(held[0], [send(held[k], "row", k) for k in range(1, rows)])

    packs = [over_row(dot_0(normed, dkv, BF).reshape(rows, feat, 2 * HD))]
    (input_grad,) = hold([input_grad], packs[0])
    input_grad = from_rows(input_grad).astype(F32)

    total = lambda t: jnp.sum(t.astype(F32), axis=0)
    fill = -feat % (2 * HD)
    place = lambda v: jnp.pad(v.reshape(rows, feat), ((0, 0), (0, fill))).reshape(rows, -1, 2 * HD)
    same = lambda v: jnp.broadcast_to(v.reshape(1, -1, 2 * HD), (rows, v.size // (2 * HD), 2 * HD))
    dq_sum = jnp.stack([total(dq[0]), total(dq[1])]).reshape(2, cols, eh)
    dq_sum = absolute([dq_sum[:, order.index(k)] for k in range(cols)], z)
    dq_sum = jnp.stack([jnp.stack(absolute([d[0], d[1]], core)) for d in dq_sum]).reshape(-1)
    up_sums = [total(dpre[0][c]) + total(dpre[1][c]) for c in (0, 1)]
    zero = jnp.zeros_like(up_sums[0])
    up_sums = absolute([up_sums[0], zero, up_sums[1], zero], z)
    up_sums = jnp.stack([jnp.stack(absolute([u, zero], core)) for u in up_sums]).reshape(-1)
    v_sum = jnp.concatenate([total(dkv[:, HD:]), jnp.zeros((HD,), F32)])
    vecs = [place(total(dn1 * xhat_one)), place(total(dn1)), place(total(dn2 * xhat_two)), place(total(dn2)),
            place(total(dmid_low)), place(total(dy)), same(dq_sum), same(up_sums), same(v_sum)]
    sizes = [v.shape[1] for v in vecs]
    pad = -sum(sizes) % 16
    vecs.append(jnp.zeros((rows, pad, 2 * HD), F32))
    packs.append(over_row(jnp.concatenate(vecs, axis=1).astype(BF)))
    pack = jnp.concatenate(packs, axis=0)
    pack = add_up(pack, [swap(pack)])
    pack = add_up(pack, [send(pack, "col", k) for k in range(1, cols)])
    packs = [pack[:feat], pack[feat:]]
    keyval_weight_grad = packs[0].astype(F32)
    pack = packs[1]
    ends, at = [], 0
    for n in sizes:
        ends.append(pack[at : at + n].astype(F32).reshape(-1))
        at += n
    return (
        block_output,
        input_grad,
        ends[0][:feat],
        ends[1][:feat],
        query_weight_grad,
        half_of(ends[6], z, 2 * eh, 0),
        keyval_weight_grad,
        ends[8][:HD],
        output_weight_grad,
        ends[4][:feat],
        ends[2][:feat],
        ends[3][:feat],
        expand_weight_grad,
        half_of(ends[7], z, 2 * fh, 0),
        shrink_weight_grad,
        ends[5][:feat],
    )


def solution(mesh):
    tokens, row, col = P(("dp", "col"), "row"), P("row"), P("col")
    tree = P("dp", None)
    return jax.shard_map(
        on_device,
        mesh=mesh,
        in_specs=(
            tokens, tokens, row, row, P("row", "col"), col, P("row", None), P(), P("col", "row"), row,
            row, row, P("row", "col"), col, P("col", "row"), row, tree, tree, tree,
        ),
        out_specs=(
            tokens, tokens, row, row, P("row", "col"), col, P("row", None), P(), P("col", "row"), row,
            row, row, P("row", "col"), col, P("col", "row"), row,
        ),
        check_vma=False,
    )
```

```python
import functools
import math

import jax
import jax.numpy as jnp
from jax import lax
from jax.experimental import pallas as pl
from jax.experimental.pallas import tpu as pltpu
from jax.sharding import PartitionSpec as P

HD = 128
TREE_TOK = 5120
TRUNK = 2048
EPSILON = 1e-05
SCALE = HD**-0.5
SCALE2 = SCALE * math.log2(math.e)
NEG = -1e30
TILE = 512
BF = jnp.bfloat16
F32 = jnp.float32
VMEM_BYTES = 60 * 1024 * 1024


def dot(a, b, out=F32):
    return jnp.dot(a, b, preferred_element_type=F32).astype(out)


def dot_t(a, b, out=F32):
    return lax.dot_general(a, b, (((1,), (1,)), ((), ())), preferred_element_type=F32).astype(out)


def dot_0(a, b, out=F32):
    return lax.dot_general(a, b, (((0,), (0,)), ((), ())), preferred_element_type=F32).astype(out)


def tail_rows(tab, i):
    return pl.ds(pl.multiple_of(tab[2, i], 128), TILE // 2), pl.ds(
        pl.multiple_of(tab[4, i], 128), TILE // 2
    )


def place_of(head, heads):
    half = heads // 2
    return head // half, slice(head % half * HD, (head % half + 1) * HD)


def fwd_kernel(tab, *refs, bs, heads, hg):
    qa_ref, qb_ref, k_ref, v_ref = refs[:4]
    oa_ref, ob_ref, lse_ref = refs[-3:]
    i = pl.program_id(0)
    full, base = tab[0, i], tab[1, i]
    lim0, lim1 = tab[3, i], tab[5, i]
    half = TILE // 2
    r0, r1 = tail_rows(tab, i)
    row = lax.broadcasted_iota(jnp.int32, (hg * bs, TILE), 0) & (bs - 1)
    col = lax.broadcasted_iota(jnp.int32, (hg * bs, TILE), 1)
    mask = col <= row + jnp.where(col < half, lim0, lim1 + half)
    for g in range(heads // hg):
        at = [place_of(g * hg + h, heads) for h in range(hg)]
        q = jnp.concatenate([(qa_ref, qb_ref)[w][:, c] for w, c in at], axis=0)
        kt = jnp.concatenate([k_ref[r0, :], k_ref[r1, :]], axis=0)
        vt = jnp.concatenate([v_ref[r0, :], v_ref[r1, :]], axis=0)
        s = jnp.where(mask, dot_t(q, kt) * SCALE2, NEG)
        top = jnp.max(s, axis=1, keepdims=True)
        acc = dot(jnp.exp2(s - top).astype(BF), vt)

        def body(t, carry):
            top, acc = carry
            rr = pl.ds(pl.multiple_of(base + t * TILE, 128), TILE)
            s = dot_t(q, k_ref[rr, :]) * SCALE2
            new = jnp.maximum(top, jnp.max(s, axis=1, keepdims=True))
            p = jnp.exp2(s - new).astype(BF)
            return new, acc * jnp.exp2(top - new) + dot(p, v_ref[rr, :])

        top, acc = lax.fori_loop(0, full, body, (top, acc))
        total = acc[:, HD:]
        out = (acc[:, :HD] / total).astype(BF)
        lse = top + jnp.log2(total)
        for h in range(hg):
            (oa_ref, ob_ref)[at[h][0]][:, at[h][1]] = out[h * bs : (h + 1) * bs]
            lse_ref[0, g * hg + h : g * hg + h + 1, :] = jnp.transpose(lse[h * bs : (h + 1) * bs])[0:1, :]


def attention_forward(tab, q, k, v_ext, blocks, *needs):
    tokens, width = q[0].shape
    bs, heads = tokens // blocks, 2 * width // HD
    qs = pl.BlockSpec((bs, width), lambda i, t: (i, 0))
    return pl.pallas_call(
        functools.partial(fwd_kernel, bs=bs, heads=heads, hg=heads),
        grid_spec=pltpu.PrefetchScalarGridSpec(
            num_scalar_prefetch=1,
            grid=(blocks,),
            in_specs=[
                qs,
                qs,
                pl.BlockSpec(k.shape, lambda i, t: (0, 0)),
                pl.BlockSpec(v_ext.shape, lambda i, t: (0, 0)),
            ]
            + [ANY] * len(needs),
            out_specs=[
                qs,
                qs,
                pl.BlockSpec((1, heads, bs), lambda i, t: (i, 0, 0)),
            ],
        ),
        out_shape=[
            jax.ShapeDtypeStruct((tokens, width), BF),
            jax.ShapeDtypeStruct((tokens, width), BF),
            jax.ShapeDtypeStruct((blocks, heads, bs), F32),
        ],
        compiler_params=pltpu.CompilerParams(vmem_limit_bytes=VMEM_BYTES),
        cost_estimate=SMALL,
        name="attn_fwd",
    )(tab, *q, k, v_ext, *needs)


def bwd_kernel(tab, *refs, bs, heads, hg, more):
    qa_ref, qb_ref, daa_ref, dab_ref, aa_ref, ab_ref, lse_ref, k_ref, v_ref = refs[:9]
    dqa_ref, dqb_ref, dkv_ref = refs[-3:]
    i = pl.program_id(0)
    full, base = tab[0, i], tab[1, i]
    lim0, lim1 = tab[3, i], tab[5, i]
    half = TILE // 2
    r0, r1 = tail_rows(tab, i)
    row = lax.broadcasted_iota(jnp.int32, (TILE, hg * bs), 1) & (bs - 1)
    col = lax.broadcasted_iota(jnp.int32, (TILE, hg * bs), 0)
    mask = col <= row + jnp.where(col < half, lim0, lim1 + half)

    @pl.when(i == 0)
    def _():
        dkv_ref[...] = refs[9][...] if more else jnp.zeros_like(dkv_ref)

    for g in range(heads // hg):
        at = [place_of(g * hg + h, heads) for h in range(hg)]
        q = jnp.concatenate([(qa_ref, qb_ref)[w][:, c] for w, c in at], axis=0)
        da = jnp.concatenate([(daa_ref, dab_ref)[w][:, c] for w, c in at], axis=0)
        lse = jnp.concatenate([lse_ref[0, g * hg + h : g * hg + h + 1, :] for h in range(hg)], axis=1)
        delta = jnp.concatenate(
            [
                jnp.sum(
                    jnp.transpose((daa_ref, dab_ref)[w][:, c].astype(F32) * (aa_ref, ab_ref)[w][:, c].astype(F32)),
                    axis=0,
                    keepdims=True,
                )
                for w, c in at
            ],
            axis=1,
        )

        def tile(kt, vt, visible):
            st = dot_t(kt, q) * SCALE2 - lse
            if visible is not None:
                st = jnp.where(visible, st, NEG)
            pt = jnp.exp2(st)
            dst = (pt * (dot_t(vt, da) - delta)).astype(BF)
            return dot(dst, q) * SCALE, dot(pt.astype(BF), da), dot_0(dst, kt)

        kt = jnp.concatenate([k_ref[r0, :], k_ref[r1, :]], axis=0)
        vt = jnp.concatenate([v_ref[r0, :], v_ref[r1, :]], axis=0)
        dk, dv, dq = tile(kt, vt, mask)
        dkv_ref[r0, :HD] += dk[:half]
        dkv_ref[r0, HD:] += dv[:half]
        dkv_ref[r1, :HD] += dk[half:]
        dkv_ref[r1, HD:] += dv[half:]

        def body(t, dq):
            rr = pl.ds(pl.multiple_of(base + t * TILE, 128), TILE)
            dk, dv, more = tile(k_ref[rr, :], v_ref[rr, :], None)
            dkv_ref[rr, :HD] += dk
            dkv_ref[rr, HD:] += dv
            return dq + more

        dq = (lax.fori_loop(0, full, body, dq) * SCALE).astype(BF)
        for h in range(hg):
            (dqa_ref, dqb_ref)[at[h][0]][:, at[h][1]] = dq[h * bs : (h + 1) * bs]


def attention_backward(tab, q, da, a, lse, k, v, blocks, first, count, so_far, *needs):
    tokens, width = q[0].shape
    bs, heads = tokens // blocks, 2 * width // HD
    qs = pl.BlockSpec((bs, width), lambda i, t: (i + first, 0))
    ks = pl.BlockSpec(k.shape, lambda i, t: (0, 0))
    whole = pl.BlockSpec((k.shape[0], 2 * HD), lambda i, t: (0, 0))
    out = pl.BlockSpec((bs, width), lambda i, t: (i, 0))
    more = [] if so_far is None else [so_far]
    return pl.pallas_call(
        functools.partial(bwd_kernel, bs=bs, heads=heads, hg=heads, more=bool(more)),
        grid_spec=pltpu.PrefetchScalarGridSpec(
            num_scalar_prefetch=1,
            grid=(count,),
            in_specs=[qs] * 6
            + [pl.BlockSpec((1, heads, bs), lambda i, t: (i + first, 0, 0)), ks, ks]
            + [whole] * len(more)
            + [ANY] * len(needs),
            out_specs=[out, out, whole],
        ),
        out_shape=[
            jax.ShapeDtypeStruct((count * bs, width), BF),
            jax.ShapeDtypeStruct((count * bs, width), BF),
            jax.ShapeDtypeStruct((k.shape[0], 2 * HD), F32),
        ],
        compiler_params=pltpu.CompilerParams(vmem_limit_bytes=VMEM_BYTES),
        cost_estimate=SMALL,
        name="attn_bwd",
    )(tab[:, first : first + count], *q, *da, *a, lse, k, v, *more, *needs)


def block_table(parent, start, places):
    slots = jnp.arange(parent.shape[0], dtype=jnp.int32)
    length = jnp.where(parent < 0, TRUNK, TILE // 2)
    mine = (places[:, None] >= start[None, :]) & (places[:, None] < (start + length)[None, :])
    pick = lambda sel, vals: jnp.sum(jnp.where(sel, vals[None, :], 0), axis=1)
    seg = pick(mine, slots)
    own = pick(mine, start)
    par = pick(mine, parent)
    is_par = slots[None, :] == par[:, None]
    par_start = pick(is_par, start)
    grand = jnp.where(par < 0, -1, pick(is_par, parent))
    trunk = jnp.sum(jnp.where(parent < 0, start, 0))
    off = places - own
    in_trunk, leaf = par < 0, grand >= 0
    full = jnp.where(in_trunk, off // TILE, TRUNK // TILE)
    half = TILE // 2
    first = jnp.where(in_trunk, trunk + full * TILE, jnp.where(leaf, par_start, own))
    lim_first = jnp.where(in_trunk, off - full * TILE, jnp.where(leaf, 2 * TILE, off))
    second = jnp.where(in_trunk, trunk + full * TILE + half, own)
    lim_second = jnp.where(in_trunk, off - full * TILE - half, jnp.where(leaf, off, -2 * TILE))
    return jnp.stack([full, jnp.full_like(full, trunk), first, lim_first, second, lim_second]).astype(jnp.int32)


SMALL = pl.CostEstimate(flops=1_000_000, bytes_accessed=1_000_000, transcendentals=0)
ANY = pl.BlockSpec(memory_space=pl.ANY)


def hold(values, *needs):
    values = list(values)
    n, m = len(values), len(needs)
    out = pl.pallas_call(
        lambda *refs: None,
        in_specs=[ANY] * (n + m),
        out_specs=[ANY] * n,
        out_shape=[jax.ShapeDtypeStruct(v.shape, v.dtype) for v in values],
        input_output_aliases={i: i for i in range(n)},
        cost_estimate=SMALL,
        name="hold",
    )(*values, *needs)
    return list(out)


def up_kernel(*refs, half, step):
    xa, xb, ya, yb, w, b = refs[:6]
    g_ref, du_ref = refs[-2:]

    def go(x, y):
        for j in range(0, w.shape[2], step):
            c = slice(j, j + step)
            u = dot(x[...], w[0, :, c]) + b[:, c]
            d = dot(y[...], w[1, :, c])
            g, slope = gelu_both(u)
            g_ref[:, c] = g.astype(BF)
            du_ref[:, c] = (d * slope).astype(BF)

    pl.when(pl.program_id(0) < half)(lambda: go(xa, ya))
    pl.when(pl.program_id(0) >= half)(lambda: go(xb, yb))


def up(x, dy, w, b, *needs):
    tokens, width = x[0].shape
    hidden = w.shape[2]
    tm, half = tokens // 2, 2
    first = pl.BlockSpec((tm, width), lambda i: (jnp.minimum(i, half - 1), 0))
    second = pl.BlockSpec((tm, width), lambda i: (jnp.maximum(i - half, 0), 0))
    return pl.pallas_call(
        functools.partial(up_kernel, half=half, step=512),
        grid=(2 * half,),
        in_specs=[first, second, first, second, pl.BlockSpec(w.shape, lambda i: (0, 0, 0)), pl.BlockSpec((1, hidden), lambda i: (0, 0))]
        + [ANY] * len(needs),
        out_specs=[pl.BlockSpec((tm, hidden), lambda i: (i, 0))] * 2,
        out_shape=[jax.ShapeDtypeStruct((2 * tokens, hidden), BF)] * 2,
        compiler_params=pltpu.CompilerParams(vmem_limit_bytes=VMEM_BYTES),
        cost_estimate=SMALL,
        name="hidden_up",
    )(*x, *dy, w, b, *needs)


def down_kernel(*refs, half, step):
    la, lb, wa, wb = refs[:4]
    own, other = refs[-2:]

    def go(o):
        for j in range(0, o.shape[1], step):
            c = slice(j, j + step)
            o[:, c] = (dot_t(la[...], wa[0, c, :]) + dot_t(lb[...], wb[0, c, :])).astype(o.dtype)

    pl.when(pl.program_id(0) < half)(lambda: go(own))
    pl.when(pl.program_id(0) >= half)(lambda: go(other))


def down(left, weights, which, *needs):
    rows, hidden = left[0].shape
    width = weights[0].shape[1]
    half = 2
    tm = rows // 4
    lefts = pl.BlockSpec((tm, hidden), lambda i: (i, 0))
    ws = pl.BlockSpec((1, width, hidden), lambda i: (which, 0, 0))
    return pl.pallas_call(
        functools.partial(down_kernel, half=half, step=512),
        grid=(2 * half,),
        in_specs=[lefts, lefts, ws, ws] + [ANY] * len(needs),
        out_specs=[
            pl.BlockSpec((tm, width), lambda i: (jnp.minimum(i, half - 1), 0)),
            pl.BlockSpec((tm, width), lambda i: (jnp.maximum(i - half, 0), 0)),
        ],
        out_shape=[jax.ShapeDtypeStruct((rows // 2, width), F32), jax.ShapeDtypeStruct((rows // 2, width), BF)],
        compiler_params=pltpu.CompilerParams(vmem_limit_bytes=VMEM_BYTES),
        cost_estimate=SMALL,
        name="hidden_down",
    )(*left, *weights, *needs)


def grads_kernel(*refs):
    xs, ys, dus, gs, o_ref = refs[:4], refs[4:8], refs[8:10], refs[10:12], refs[-1]

    def go(left, right):
        lhs = jnp.concatenate([r[...] for r in left], axis=0)
        rhs = jnp.concatenate([r[...] for r in right], axis=0)
        o_ref[0] = dot_0(lhs, rhs).astype(BF)

    pl.when(pl.program_id(0) == 0)(lambda: go(xs, dus))
    pl.when(pl.program_id(0) == 1)(lambda: go(ys, gs))


def weight_grads(x, dy, du, g, *needs):
    tokens, width = x[0].shape
    hidden = du[0].shape[1]
    tm = min(256, width)
    last = width // tm - 1
    xs = pl.BlockSpec((tokens, tm), lambda j, i: (0, jnp.where(j == 0, i, last)))
    ys = pl.BlockSpec((tokens, tm), lambda j, i: (0, jnp.where(j == 0, 0, i)))
    rs = pl.BlockSpec((2 * tokens, hidden), lambda j, i: (0, 0))
    return pl.pallas_call(
        grads_kernel,
        grid=(2, width // tm),
        in_specs=[xs] * 4 + [ys] * 4 + [rs] * 4 + [ANY] * len(needs),
        out_specs=pl.BlockSpec((1, tm, hidden), lambda j, i: (j, i, 0)),
        out_shape=jax.ShapeDtypeStruct((2, width, hidden), BF),
        compiler_params=pltpu.CompilerParams(vmem_limit_bytes=VMEM_BYTES),
        cost_estimate=SMALL,
        name="hidden_grads",
    )(*x, *dy, *du, *g, *needs)


def normalise(x):
    mean = jnp.mean(x, axis=1, keepdims=True)
    cent = x - mean
    inv = lax.rsqrt(jnp.mean(cent * cent, axis=1, keepdims=True) + EPSILON)
    return mean, inv


def norm_back(grad, xhat, inv, gain):
    c = grad * gain
    return inv * (c - jnp.mean(c, axis=1, keepdims=True) - xhat * jnp.mean(c * xhat, axis=1, keepdims=True))


def gelu_both(u):
    k, a = math.sqrt(2 / math.pi), 0.044715
    square = u * u
    t = jnp.tanh(u * (k + (k * a) * square))
    h = 0.5 * (1 + t)
    return u * h, h + (0.5 * u) * (1 - t * t) * (k + (3 * k * a) * square)


def on_device(
    block_input,
    cotangent,
    attn_gain,
    attn_shift,
    query_weight,
    query_bias,
    keyval_weight,
    value_bias,
    output_weight,
    output_bias,
    mlp_gain,
    mlp_shift,
    expand_weight,
    expand_bias,
    shrink_weight,
    shrink_bias,
    seg_parent,
    seg_start,
    seg_length,
):
    rows, cols = lax.axis_size("row"), lax.axis_size("col")
    core, me, z = lax.axis_index("dp"), lax.axis_index("row"), lax.axis_index("col")
    local, feat = block_input.shape
    width = feat * rows
    tokens = local // rows
    bs = math.gcd(tokens, 128)
    blocks = tokens // bs
    eh = query_weight.shape[1] // 2
    fh = expand_weight.shape[1] // 2
    order = (0, 2, 1, 3)

    def send(x, axis, bits):
        n = lax.axis_size(axis)
        return lax.ppermute(x, axis, [(i, i ^ bits) for i in range(n)])

    swap = lambda x: send(x, "dp", 1)
    z_one = lambda x: send(x, "col", 1)
    z_two = lambda x: send(x, "col", 2)
    half_of = lambda x, c, size, axis: lax.dynamic_slice_in_dim(x, c * size, size, axis)

    def absolute(parts, index):
        bit = 1
        while bit < len(parts):
            odd = (index & bit) != 0
            parts = [jnp.where(odd, parts[j ^ bit], parts[j]) for j in range(len(parts))]
            bit *= 2
        return parts

    def to_rows(x, needs=(), then=()):
        x = x.reshape(blocks, rows, bs, feat)
        parts = [lax.dynamic_index_in_dim(x, me ^ k, 1, False).reshape(tokens, feat) for k in range(rows)]
        if needs:
            parts = hold(parts, *needs)
        parts = parts[:1] + [send(parts[k], "row", k) for k in range(1, rows)]
        return parts

    def from_rows(x):
        piece = lambda k: half_of(x, me ^ k, feat, 1)
        parts = [piece(0)] + [send(piece(k), "row", k) for k in range(1, rows)]
        parts = [p.reshape(blocks, 1, bs, feat) for p in absolute(parts, me)]
        return jnp.concatenate(parts, axis=1).reshape(local, feat)

    def by_core(own, other, axis):
        return jnp.where(
            core == 0, jnp.concatenate([own, other], axis), jnp.concatenate([other, own], axis)
        )

    x_parts = to_rows(block_input)
    x_low = jnp.concatenate(absolute(x_parts, me), axis=1)
    x = x_low.astype(F32)

    vectors = jnp.stack([attn_gain, attn_shift, output_bias, mlp_gain, mlp_shift, shrink_bias] + [attn_gain] * 2)
    packed = jnp.concatenate([keyval_weight, vectors.reshape(-1, 2 * HD)], axis=0)
    packed = [packed] + [send(packed, "row", k) for k in range(1, rows)]
    packs = packed[1:]
    packed = jnp.stack(absolute(packed, me))
    up_bias = half_of(expand_bias, core, fh, 0).astype(F32)[None]
    up_bias = [up_bias, z_two(up_bias)]
    kv_weight = packed[:, :feat].reshape(width, 2 * HD)
    vectors = packed[:, feat:].reshape(rows, 8, feat).transpose(1, 0, 2).reshape(8, width).astype(F32)
    gain_one, shift_one, out_bias, gain_two, shift_two, down_bias = (vectors[i : i + 1] for i in range(6))

    gather_rows = lambda w, axis=0: lax.all_gather(w, "row", axis=axis, tiled=True)

    def four(block):
        return [block] + [send(block, "col", k) for k in order[1:]]

    q_parts = four(query_bias)
    q_bias = jnp.stack(q_parts).reshape(cols, 2, eh).astype(F32)
    q_bias = [lax.dynamic_index_in_dim(q_bias, c, 1, False).reshape(1, cols * eh) for c in (core, 1 - core)]

    def gather_square(four_blocks):
        own = gather_rows(jnp.concatenate(four_blocks, axis=1))
        return own, swap(own)

    query_blocks = four(half_of(query_weight, core, eh, 1))
    out_blocks = four(half_of(output_weight, core, eh, 0).T)
    hidden = jnp.stack([half_of(expand_weight, core, fh, 1), half_of(shrink_weight, core, fh, 0).T])
    pieces = [z_two(p) for p in jnp.split(hidden, 8, axis=2)]
    query_blocks[1:] = hold(query_blocks[1:], x_parts[-1], pieces[0])
    wq_own = gather_rows(jnp.concatenate(query_blocks, axis=1))
    dy_parts = to_rows(cotangent, [x_low])


    mean_one, inv_one = normalise(x)
    normed = ((x - mean_one) * inv_one * gain_one + shift_one).astype(BF)
    kv_shift = jnp.concatenate([jnp.zeros((HD,), F32), value_bias.astype(F32)])[None]
    kv = (dot(normed, kv_weight) + kv_shift).astype(BF)
    odd = z % 2
    kv_pair = jnp.stack(absolute([kv, z_one(kv)], odd))
    halves = hold([kv_pair[:, : tokens // 2], kv_pair[:, tokens // 2 :]], pieces[1], pieces[2], dy_parts[-1], up_bias[1], *q_parts[1:])
    halves = [[h] for h in halves]
    bits = [1 << i for i in range(rows.bit_length() - 1)]
    for step in range(len(bits)):
        for h, turn in ((0, bits), (1, bits[::-1])):
            halves[h] = halves[h] + [send(p, "row", turn[step]) for p in halves[h]]
        if step == 0:
            n = len(halves[0])
            both = hold(halves[0] + halves[1], pieces[3], dy_parts[1])
            halves = [both[:n], both[n:]]
    flip = lambda turn: [sum(turn[b] for b in range(len(bits)) if (i >> b) & 1) for i in range(rows)]
    for h, turn in ((0, bits), (1, bits[::-1])):
        held = flip(turn)
        halves[h] = jnp.stack(absolute([halves[h][held.index(k)] for k in range(rows)], me))
    kv_all = jnp.concatenate(halves, axis=2)
    kv_all = kv_all.reshape(rows, 2, blocks, bs, 2 * HD).transpose(1, 2, 0, 3, 4).reshape(2 * local, 2 * HD)
    keys, values = kv_all[:, :HD], kv_all[:, HD:]
    out_blocks[1:] = hold(out_blocks[1:], keys)
    wo_t = gather_square(out_blocks)
    hidden_near = hold([half_of(expand_weight, core, fh, 1), half_of(shrink_weight, core, fh, 0).T], out_blocks[1])
    hidden_near = gather_rows(jnp.stack(hidden_near), 1)
    (wq_own,) = hold([wq_own], keys, pieces[4], *dy_parts[2:-1])
    wq = [wq_own, swap(wq_own)]
    q = [(dot(normed, w) + v).astype(BF) for w, v in zip(wq, q_bias)]

    dy = jnp.concatenate(absolute(dy_parts, me), axis=1)
    dy_far = z_one(dy)

    tree = z // 2
    tree_row = lambda t: lax.dynamic_index_in_dim(t, tree, 0, False)
    places = odd * local + (jnp.arange(blocks, dtype=jnp.int32) * rows + me) * bs
    tab = block_table(tree_row(seg_parent), tree_row(seg_start), places)
    v_ext = jnp.concatenate([values, jnp.ones_like(values)], axis=1)
    *att, lse = attention_forward(tab, q, keys, v_ext, blocks, dy, pieces[5])
    *pieces[6:], dy_far = hold(pieces[6:] + [dy_far], att[0])
    hidden_z = jnp.concatenate(pieces, axis=2)
    hidden_w = [hidden_near, gather_rows(hidden_z, 1)]
    mid = x + dot_t(att[0], wo_t[0]) + dot_t(att[1], wo_t[1]) + out_bias

    mean_two, inv_two = normalise(mid)
    xhat_two = (mid - mean_two) * inv_two
    normed_two = (xhat_two * gain_two + shift_two).astype(BF)
    n2_far = z_one(normed_two)
    n2 = [(normed_two, swap(normed_two)), None]
    dy_all = [(dy, swap(dy)), None]
    act, dpre = [[None] * 2, [None] * 2], [[None] * 2, [None] * 2]
    scatter_rows = lambda w, axis=0: lax.psum_scatter(w, "row", scatter_dimension=axis, tiled=True)
    grads, last = [None] * 2, []
    for c in range(2):
        for a in range(2):
            act[a][c], dpre[a][c] = up(n2[a], dy_all[a], hidden_w[c], up_bias[c], *last)
            last = [dpre[a][c]]
            if n2[1] is None:
                (n2_far,) = hold([n2_far], dpre[0][0])
                n2[1] = (n2_far, swap(n2_far))
                dy_all[1] = (dy_far, swap(dy_far))
        if c == 1:
            dn2_own, dn2_other = down(dpre[1], hidden_w, 0)
            dn2_far = (dn2_own + swap(dn2_other).astype(F32)).astype(BF)
            dn2_own, dn2_other = down(dpre[0], hidden_w, 0, dn2_own)
            (dn2_far,) = hold([dn2_far], dn2_own)
            last = [dn2_far]
            dn2_far = z_one(dn2_far)
        grads[c] = weight_grads(n2[0] + n2[1], dy_all[0] + dy_all[1], [d[c] for d in dpre], [g[c] for g in act], *last)
        last = [grads[c]]
    d_hidden_near = scatter_rows(grads[0], 1)
    (grads[1],) = hold([grads[1]], d_hidden_near)
    d_hidden_far = scatter_rows(grads[1], 1)
    branch_own, branch_other = down(act[1], hidden_w, 1, grads[1])
    near_own, near_other = down(act[0], hidden_w, 1, branch_own)
    (dn2_far,) = hold([dn2_far], near_own)
    dn2 = dn2_own + swap(dn2_other).astype(F32) + dn2_far.astype(F32)
    (branch_far,) = hold([(branch_own + swap(branch_other).astype(F32)).astype(BF)], dn2_far)
    branch_far = z_one(branch_far)
    branch_near = near_own + swap(near_other).astype(F32)

    dmid = dy.astype(F32) + norm_back(dn2, xhat_two, inv_two, gain_two)
    dmid_low = dmid.astype(BF)
    datt = [dot(dmid_low, w, BF) for w in wo_t]

    def halve(x, axis, mesh_axis, bits):
        parts = jnp.split(x, len(bits), axis=axis)
        got = [send(p, mesh_axis, b) for p, b in zip(parts[1:], bits[1:])]
        return sum((g.astype(F32) for g in got), parts[0].astype(F32)).astype(BF)

    def square_part(left, right):
        other = dot_0(left, right[1], BF)
        return (dot_0(left, right[0]) + swap(other).astype(F32)).astype(BF), other

    d_out = scatter_rows(square_part(dmid_low, att)[0])
    cut = blocks - 1
    *dq_a, dkv_part = attention_backward(tab, q, datt, att, lse, keys, values, blocks, 0, cut, None, d_hidden_far)
    d_hidden_got = z_two(d_hidden_far)
    *dq_b, dkv_part = attention_backward(tab, q, datt, att, lse, keys, values, blocks, cut, blocks - cut, dkv_part, d_hidden_got)
    dq = [jnp.concatenate([u, v]) for u, v in zip(dq_a, dq_b)]
    d_hidden = d_hidden_near.astype(F32) + d_hidden_got.astype(F32)
    d_hidden = d_hidden.astype(BF)
    d_up, d_down = d_hidden[0], d_hidden[1]
    expand_weight_grad = by_core(d_up, swap(d_up), 1).astype(F32)
    shrink_weight_grad = by_core(d_down.T, swap(d_down.T), 0).astype(F32)

    (branch_far,) = hold([branch_far], dq_b[0])
    branch = branch_near + branch_far.astype(F32)
    block_output = from_rows((mid + branch + down_bias).astype(BF))
    d_query, d_query_other = square_part(normed, dq)
    d_query = scatter_rows(d_query)
    parts = dkv_part.astype(BF).reshape(2, blocks, rows, bs, 2 * HD)
    pair = lambda k: lax.dynamic_index_in_dim(parts, odd ^ k, 0, False)
    dkv_sum = pair(0).astype(F32) + z_one(pair(1)).astype(F32)
    dkv_sum = dkv_sum.astype(BF)
    relative = lambda k: lax.dynamic_index_in_dim(dkv_sum, me ^ k, 1, False).reshape(tokens, 2 * HD)
    done = []
    for h, turn in ((0, bits), (1, bits[::-1])):
        cut = slice(h * tokens // 2, (h + 1) * tokens // 2)
        held = [relative(k)[cut] for k in flip(turn[::-1])]
        for step in range(len(bits)):
            n = len(held) // 2
            got = [send(p, "row", turn[::-1][len(bits) - 1 - step]) for p in held[n:]]
            held = [(p.astype(F32) + g.astype(F32)).astype(BF) for p, g in zip(held[:n], got)]
        done.append(held[0])
    dkv = jnp.concatenate(done, axis=0)
    (d_out,) = hold([d_out], dkv)
    d_out = halve(d_out, 1, "col", order)
    output_weight_grad = by_core(d_out.T, swap(d_out.T), 0).astype(F32)
    d_query = halve(d_query, 1, "col", order)
    query_weight_grad = by_core(d_query, swap(d_query), 1).astype(F32)

    (dkv,) = hold([dkv], block_output)
    dn1 = dot_t(dq[0], wq[0]) + dot_t(dq[1], wq[1]) + dot_t(dkv, kv_weight)
    xhat_one = (x - mean_one) * inv_one
    input_grad = (dmid + norm_back(dn1, xhat_one, inv_one, gain_one)).astype(BF)
    add_up = lambda first, others: sum((o.astype(F32) for o in others), first.astype(F32)).astype(BF)

    def over_row(pack):
        held = [lax.dynamic_index_in_dim(pack, me ^ k, 0, False) for k in range(rows)]
        return add_up(held[0], [send(held[k], "row", k) for k in range(1, rows)])

    packs = [over_row(dot_0(normed, dkv, BF).reshape(rows, feat, 2 * HD))]
    (input_grad,) = hold([input_grad], packs[0])
    input_grad = from_rows(input_grad).astype(F32)

    total = lambda t: jnp.sum(t.astype(F32), axis=0)
    fill = -feat % (2 * HD)
    place = lambda v: jnp.pad(v.reshape(rows, feat), ((0, 0), (0, fill))).reshape(rows, -1, 2 * HD)
    same = lambda v: jnp.broadcast_to(v.reshape(1, -1, 2 * HD), (rows, v.size // (2 * HD), 2 * HD))
    dq_sum = jnp.stack([total(dq[0]), total(dq[1])]).reshape(2, cols, eh)
    dq_sum = absolute([dq_sum[:, order.index(k)] for k in range(cols)], z)
    dq_sum = jnp.stack([jnp.stack(absolute([d[0], d[1]], core)) for d in dq_sum]).reshape(-1)
    up_sums = [total(dpre[0][c]) + total(dpre[1][c]) for c in (0, 1)]
    zero = jnp.zeros_like(up_sums[0])
    up_sums = absolute([up_sums[0], zero, up_sums[1], zero], z)
    up_sums = jnp.stack([jnp.stack(absolute([u, zero], core)) for u in up_sums]).reshape(-1)
    v_sum = jnp.concatenate([total(dkv[:, HD:]), jnp.zeros((HD,), F32)])
    vecs = [place(total(dn1 * xhat_one)), place(total(dn1)), place(total(dn2 * xhat_two)), place(total(dn2)),
            place(total(dmid_low)), place(total(dy)), same(dq_sum), same(up_sums), same(v_sum)]
    sizes = [v.shape[1] for v in vecs]
    pad = -sum(sizes) % 16
    vecs.append(jnp.zeros((rows, pad, 2 * HD), F32))
    packs.append(over_row(jnp.concatenate(vecs, axis=1).astype(BF)))
    pack = jnp.concatenate(packs, axis=0)
    pack = add_up(pack, [swap(pack)])
    pack = add_up(pack, [send(pack, "col", k) for k in range(1, cols)])
    packs = [pack[:feat], pack[feat:]]
    keyval_weight_grad = packs[0].astype(F32)
    pack = packs[1]
    ends, at = [], 0
    for n in sizes:
        ends.append(pack[at : at + n].astype(F32).reshape(-1))
        at += n
    return (
        block_output,
        input_grad,
        ends[0][:feat],
        ends[1][:feat],
        query_weight_grad,
        half_of(ends[6], z, 2 * eh, 0),
        keyval_weight_grad,
        ends[8][:HD],
        output_weight_grad,
        ends[4][:feat],
        ends[2][:feat],
        ends[3][:feat],
        expand_weight_grad,
        half_of(ends[7], z, 2 * fh, 0),
        shrink_weight_grad,
        ends[5][:feat],
    )


def solution(mesh):
    tokens, row, col = P(("dp", "col"), "row"), P("row"), P("col")
    tree = P("dp", None)
    return jax.shard_map(
        on_device,
        mesh=mesh,
        in_specs=(
            tokens, tokens, row, row, P("row", "col"), col, P("row", None), P(), P("col", "row"), row,
            row, row, P("row", "col"), col, P("col", "row"), row, tree, tree, tree,
        ),
        out_specs=(
            tokens, tokens, row, row, P("row", "col"), col, P("row", None), P(), P("col", "row"), row,
            row, row, P("row", "col"), col, P("col", "row"), row,
        ),
        check_vma=False,
    )
```
